256 devices in a mesh: grp: 8 (over y, x_lo), blk: 32 (over z, x_hi, core).
Axes of the slice: x: 4 (x_hi: 2, x_lo: 2; x = x_hi * 2 + x_lo), y: 4, z: 8, core: 2. Of those that a mesh axis runs over, the one named last changes fastest.
Arguments:
- sources: bfloat16 [32768, 768], P('blk'), may hold values from -1 to 1
- targets: bfloat16 [16384, 768], P(('grp', 'blk')), may hold values from -1 to 1
- potential_in: float32 [16384], P(('grp', 'blk')), may hold values from -6 to 6
- source_logw: float32 [32768], P('blk'), may hold values from -12 to 12
- target_logw: float32 [16384], P(('grp', 'blk')), may hold values from -12 to 12
Outputs:
- source_potential: float32 [32768], P('blk')
- potential_out: float32 [16384], P(('grp', 'blk'))
The draws below stay inside these ranges and needn't reach their ends.
All inputs are finite; a program needn't handle non-finite values.
Results may differ from the reference program's by a relative error of at most 0.0003.
Values may be sent and summed in bfloat16 or wider, within the bound.
No kernel may reach another device: no remote copies, remote signals or barrier semaphores. Data moves between devices by JAX's collectives and lax.ppermute only.
A program may use at most 64 MiB of HBM per device.

```python
import math
import jax
import jax.numpy as jnp
from jax import lax

D = 768
SRC_DEV = 1024
TGT_DEV = 64
M = 32768
N = 16384


def embed_rows(key, rows, lower, upper):
    first, second = jax.random.split(key)
    values = jax.random.truncated_normal(first, -5.0, 5.0, (rows, D), jnp.float32)
    scales = jnp.exp(jax.random.uniform(second, (rows, 1), jnp.float32, math.log(lower), math.log(upper)))
    return values * scales / math.sqrt(D)


def target_pool(key, lower, upper):
    return embed_rows(jax.random.fold_in(key, 11), N, lower, upper)


def draw_targets(key, part):
    pool = target_pool(key, 0.5, 2.0)
    return jnp.clip(pool, -1.0, 1.0).astype(jnp.bfloat16)


def draw_sources(key, part):
    key = jax.random.fold_in(key, 5)
    own = embed_rows(key, M, 0.5, 2.0)
    return jnp.clip(own, -1.0, 1.0).astype(jnp.bfloat16)


def levels(key, dims, cuts, low, largest):
    def one(axis_at, shards_of):
        steps = jax.random.uniform(jax.random.fold_in(jax.random.fold_in(key, 6), axis_at), (shards_of,), jnp.float32, low / len(cuts), largest / len(cuts))
        return jnp.repeat(jnp.exp(steps), dims[axis_at] // shards_of).reshape((-1,) + (1,) * (len(dims) - axis_at - 1))

    loudness = one(*cuts[0])
    for cut in cuts[1:]:
        loudness = loudness * one(*cut)
    return loudness


def centred(key, shape, width, most, cuts=(), kind=jnp.bfloat16):
    array = jax.random.normal(key, shape, jnp.float32) * width
    if len(cuts) > 0:
        array = levels(key, shape, cuts, -0.22, 0.18) * array
    return jnp.clip(array, min=-most, max=most).astype(kind)


def setup_inputs(seed: int = 0) -> dict:
    seeds = jax.random.split(jax.random.key(seed), 6)
    return {
        "sources": draw_sources(jax.random.fold_in(seeds[5], 71), 0),
        "targets": draw_targets(jax.random.fold_in(seeds[5], 71), 0),
        "potential_in": centred(seeds[2], (N,), 1.0, 6.0, ((0, 256),), jnp.float32),
        "source_logw": centred(seeds[3], (M,), 3.0, 12.0, ((0, 32),), jnp.float32),
        "target_logw": centred(seeds[4], (N,), 3.0, 12.0, ((0, 256),), jnp.float32),
    }


EPSILON = 0.05


def log_sum(scores):
    peak = jnp.max(scores, axis=1)
    return peak + jnp.log(jnp.sum(jnp.exp(scores - peak[:, None]), axis=1))


def reference(sources, targets, potential_in, source_logw, target_logw):
    src_sq = jnp.sum(jnp.square(sources.astype(jnp.float32)), axis=1)
    tgt_sq = jnp.sum(jnp.square(targets.astype(jnp.float32)), axis=1)
    src_blocks = sources.reshape(M // SRC_DEV, SRC_DEV, D)
    src_sq_blocks = src_sq.reshape(M // SRC_DEV, SRC_DEV)

    def row_block(pieces):
        block, block_sq = pieces
        cross = lax.dot_general(block, targets, (((1,), (1,)), ((), ())), preferred_element_type=jnp.float32)
        scores = target_logw[None, :] + (potential_in[None, :] - tgt_sq[None, :] + 2.0 * cross - block_sq[:, None]) / EPSILON
        return -EPSILON * log_sum(scores)

    source_potential = lax.map(row_block, (src_blocks, src_sq_blocks)).reshape(M)
    tgt_blocks = targets.reshape(N // TGT_DEV, TGT_DEV, D)
    tgt_sq_blocks = tgt_sq.reshape(N // TGT_DEV, TGT_DEV)

    def col_block(pieces):
        block, block_sq = pieces
        cross = lax.dot_general(block, sources, (((1,), (1,)), ((), ())), preferred_element_type=jnp.float32)
        scores = source_logw[None, :] + (source_potential[None, :] - src_sq[None, :] + 2.0 * cross - block_sq[:, None]) / EPSILON
        return -EPSILON * log_sum(scores)

    potential_out = lax.map(col_block, (tgt_blocks, tgt_sq_blocks)).reshape(N)
    return source_potential, potential_out
```

```python
import math

import jax
import jax.numpy as jnp
from jax import lax
from jax.experimental import pallas as pl
from jax.experimental.pallas import tpu as pltpu
from jax.sharding import Mesh, PartitionSpec as P

EPSILON = 0.05
LOG2E = math.log2(math.e)
SCALE = 2.0 / EPSILON * LOG2E
BACK = EPSILON * math.log(2.0)

D = 768
PAD = 128
UNIT = 128
UNITS = 8
ROWS = UNIT * UNITS
SRC = 2048
BLOCK = 512
PLANE = 16
OFFSETS = (1, -1, 2, -2, 3, -3, 0, 4)
VMEM = 48 * 1024 * 1024


def ring(value, step):
    count = lax.axis_size("z")
    return lax.ppermute(value, "z", [(i, (i + step) % count) for i in range(count)])


def other_core(value):
    return lax.ppermute(value, "core", [(0, 1), (1, 0)])


def facing(value):
    return lax.ppermute(value, ("x_lo", "x_hi"), [(0, 3), (3, 0), (1, 2), (2, 1)])


def log_sum2(values):
    peak = jnp.max(values, axis=0, keepdims=True)
    return peak + jnp.log2(jnp.sum(jnp.exp2(values - peak), axis=0, keepdims=True))


def row_kernel(units, last, *refs):
    group_refs = refs[:units]
    src_ref = refs[units]
    rest = refs[units + 1 :]
    cross_ref, lse_ref = rest[-2:]
    parts = []
    for at, group_ref in enumerate(group_refs):
        cross = lax.dot_general(
            group_ref[:, :D],
            src_ref[...],
            (((1,), (1,)), ((), ())),
            preferred_element_type=jnp.float32,
        )
        cross = cross * SCALE
        cross_ref[at * UNIT : (at + 1) * UNIT, :] = cross
        pieces = group_ref[:, D : D + PAD].astype(jnp.float32)
        bias = pieces[:, 0:1] + pieces[:, 1:2] + pieces[:, 2:3]
        parts.append(cross + bias)
    scores = parts[0] if units == 1 else jnp.concatenate(parts, axis=0)
    total = log_sum2(scores)
    if last:
        earlier = [ref[...] for ref in rest[1:-2]]
        total = log_sum2(jnp.concatenate([total, *earlier], axis=0))
        total = jnp.broadcast_to(total, (PLANE, BLOCK))
    lse_ref[...] = total


def row_pass(groups, sources, buffer, place, earlier=()):
    units = len(groups)
    last = len(earlier) > 0
    rows = units * UNIT
    in_specs = [pl.BlockSpec((UNIT, D + PAD), lambda i: (0, 0))] * units
    in_specs.append(pl.BlockSpec((BLOCK, D), lambda i: (i, 0)))
    operands = [*groups, sources]
    aliases = {}
    if buffer is not None:
        aliases = {len(operands): 0}
        operands.append(buffer)
        in_specs.append(pl.BlockSpec(memory_space=pl.ANY))
    elif last:
        raise ValueError("no buffer")
    for value in earlier:
        operands.append(value)
        in_specs.append(pl.BlockSpec((1, BLOCK), lambda i: (0, i)))
    height = PLANE if last else 1

    def body(*refs):
        row_kernel(units, last, *refs)

    return pl.pallas_call(
        body,
        grid=(SRC // BLOCK,),
        in_specs=in_specs,
        out_specs=[
            pl.BlockSpec((rows, BLOCK), lambda i: (place, i)),
            pl.BlockSpec((height, BLOCK), lambda i: (0, i)),
        ],
        out_shape=[
            jax.ShapeDtypeStruct((ROWS, SRC), jnp.float32),
            jax.ShapeDtypeStruct((height, SRC), jnp.float32),
        ],
        input_output_aliases=aliases,
        compiler_params=pltpu.CompilerParams(vmem_limit_bytes=VMEM),
        cost_estimate=pl.CostEstimate(
            flops=2 * rows * SRC * D,
            bytes_accessed=SRC * D * 2 + rows * SRC * 4,
            transcendentals=rows * SRC,
        ),
        name="rows",
    )(*operands)


def column_kernel(z_ref, cross_ref, partial_ref, logw_ref, out_ref, row_ref, bias_ref):
    step = pl.program_id(0)

    @pl.when(step == 0)
    def _():
        row = log_sum2(partial_ref[...])
        row_ref[...] = row
        bias_ref[...] = logw_ref[...] * LOG2E - row

    scores = cross_ref[...] + bias_ref[...]
    peak = jnp.max(scores, axis=1, keepdims=True)
    total = jnp.sum(jnp.exp2(scores - peak), axis=1, keepdims=True)
    lse = jnp.broadcast_to(peak + jnp.log2(total), (UNIT, UNIT)).T
    half = step // 2 + 1
    offset = jnp.where(step % 2 == 0, half, UNITS - half)
    offset = jnp.where(step == 6, 0, offset)
    place = lax.rem(z_ref[0] + offset, UNITS)
    out_ref[pl.ds(place, 1), :] = lse[0:1, :]


def column_pass(z, cross, partial, logw):
    return pl.pallas_call(
        column_kernel,
        grid=(UNITS,),
        in_specs=[
            pl.BlockSpec(memory_space=pltpu.SMEM),
            pl.BlockSpec((UNIT, SRC), lambda i: (i, 0)),
            pl.BlockSpec((PLANE, SRC), lambda i: (0, 0)),
            pl.BlockSpec((1, SRC), lambda i: (0, 0)),
        ],
        out_specs=[
            pl.BlockSpec((UNITS, UNIT), lambda i: (0, 0)),
            pl.BlockSpec((1, SRC), lambda i: (0, 0)),
        ],
        out_shape=[
            jax.ShapeDtypeStruct((UNITS, UNIT), jnp.float32),
            jax.ShapeDtypeStruct((1, SRC), jnp.float32),
        ],
        scratch_shapes=[pltpu.VMEM((1, SRC), jnp.float32)],
        compiler_params=pltpu.CompilerParams(vmem_limit_bytes=VMEM),
        cost_estimate=pl.CostEstimate(
            flops=6 * ROWS * SRC, bytes_accessed=ROWS * SRC * 4, transcendentals=ROWS * SRC
        ),
        name="columns",
    )(z, cross, partial, logw)


def on_device(sources, targets, potential_in, source_logw, target_logw):
    core = lax.axis_index("core")
    z = lax.axis_index("z").astype(jnp.int32).reshape(1)

    tgt_sq = jnp.sum(jnp.square(targets.astype(jnp.float32)), axis=1)
    bias = (target_logw + (potential_in - tgt_sq) / EPSILON) * LOG2E
    high = lax.reduce_precision(bias, 8, 7)
    middle = lax.reduce_precision(bias - high, 8, 7)
    low = bias - high - middle
    pieces = jnp.stack([high, middle, low], axis=1).astype(jnp.bfloat16)
    own = jnp.concatenate([targets, jnp.pad(pieces, ((0, 0), (0, PAD - 3)))], axis=1)

    pair = jnp.concatenate([own, facing(own)], axis=0)

    def both(value):
        other = other_core(value)
        first = core == 0
        return jnp.concatenate(
            [jnp.where(first, value, other), jnp.where(first, other, value)], axis=0
        )

    all_sources = both(sources)
    logw = both(source_logw).reshape(1, SRC)
    src_sq = jnp.sum(jnp.square(sources.astype(jnp.float32)), axis=1)

    lses = []
    buffer, lse = row_pass([pair], all_sources, None, 6)
    lses.append(lse)
    below = above = pair
    for step in range(3):
        below, above = ring(below, 1), ring(above, -1)
        buffer, lse = row_pass([above, below], all_sources, buffer, step)
        lses.append(lse)
    opposite = ring(below, 1)
    buffer, shared = row_pass([opposite], all_sources, buffer, 7, lses)

    partial = lax.all_to_all(shared, ("y", "x_lo", "core"), 0, 0, tiled=True)
    columns, rows = column_pass(z, buffer, partial, logw)
    mine = lax.dynamic_slice(rows.reshape(SRC), (core * (SRC // 2),), (SRC // 2,))
    source_potential = src_sq - BACK * mine

    gathered = lax.all_to_all(columns, "z", 0, 0, tiled=True)
    summed = log_sum2(gathered).reshape(UNIT)
    arrived = facing(summed[UNIT // 2 :])
    final = log_sum2(jnp.stack([summed[: UNIT // 2], arrived], axis=0)).reshape(UNIT // 2)
    potential_out = tgt_sq - BACK * final
    return (source_potential, potential_out)


def solution(mesh):
    fine = Mesh(mesh.devices.reshape(4, 2, 8, 2, 2), ("y", "x_lo", "z", "x_hi", "core"))
    blk = ("z", "x_hi", "core")
    every = ("y", "x_lo", "z", "x_hi", "core")
    in_specs = (P(blk, None), P(every, None), P(every), P(blk), P(every))
    out_specs = (P(blk), P(every))
    return jax.shard_map(
        on_device, mesh=fine, in_specs=in_specs, out_specs=out_specs, check_vma=False
    )
```

```python
import math

import jax
import jax.numpy as jnp
from jax import lax
from jax.experimental import pallas as pl
from jax.experimental.pallas import tpu as pltpu
from jax.sharding import Mesh, PartitionSpec as P

EPSILON = 0.05
LOG2E = math.log2(math.e)
SCALE = 2.0 / EPSILON * LOG2E
BACK = EPSILON * math.log(2.0)

D = 768
PAD = 128
OWN = 64
UNIT = 2 * OWN
UNITS = 8
ROWS = UNIT * UNITS
HALF = 1024
BLOCK = 256
PARTS = HALF // BLOCK
LANES = 128
PEERS = 16
STEPS = 5
VMEM = 12 * 1024 * 1024
NEAR = 640
IN_VMEM = pl.BlockSpec(memory_space=pltpu.VMEM)
IN_HBM = pl.BlockSpec(memory_space=pl.ANY)
IN_SMEM = pl.BlockSpec(memory_space=pltpu.SMEM)


def whole(*shape):
    return pl.BlockSpec(shape, lambda i: (0,) * len(shape))


def onward(value):
    count = lax.axis_size("z")
    up = [(2 * i, 2 * ((i + 1) % count)) for i in range(count)]
    down = [(2 * i + 1, 2 * ((i - 1) % count) + 1) for i in range(count)]
    return lax.ppermute(value, ("z", "core"), up + down)


def onward_across(value):
    count = lax.axis_size("z")
    up = [(2 * i + 1, 2 * ((i + 1) % count)) for i in range(count)]
    down = [(2 * i, 2 * ((i - 1) % count) + 1) for i in range(count)]
    return lax.ppermute(value, ("z", "core"), up + down)


def other_core(value):
    return lax.ppermute(value, "core", [(0, 1), (1, 0)])


def facing(value):
    return lax.ppermute(value, ("x_lo", "x_hi"), [(0, 3), (3, 0), (1, 2), (2, 1)])


def log_sum2(values):
    peak = jnp.max(values, axis=0, keepdims=True)
    return peak + jnp.log2(jnp.sum(jnp.exp2(values - peak), axis=0, keepdims=True))


def pack_kernel(tgt_ref, pot_ref, logw_ref, own_ref, sq_ref):
    tgt = tgt_ref[...]
    wide = tgt.astype(jnp.float32)
    sq = jnp.sum(wide * wide, axis=1, keepdims=True)
    diagonal = lax.broadcasted_iota(jnp.int32, (OWN, OWN), 0) == lax.broadcasted_iota(
        jnp.int32, (OWN, OWN), 1
    )

    def upright(row):
        return jnp.sum(jnp.where(diagonal, row, 0.0), axis=1, keepdims=True)

    sq_ref[...] = jnp.sum(jnp.where(diagonal, sq, 0.0), axis=0, keepdims=True)
    bias = (upright(logw_ref[...]) + (upright(pot_ref[...]) - sq) / EPSILON) * LOG2E
    high = bias.astype(jnp.bfloat16)
    rest = bias - high.astype(jnp.float32)
    middle = rest.astype(jnp.bfloat16)
    low = rest - middle.astype(jnp.float32)
    lane = lax.broadcasted_iota(jnp.int32, (OWN, PAD), 1)
    pieces = jnp.where(lane == 0, high.astype(jnp.float32), 0.0)
    pieces = jnp.where(lane == 1, middle.astype(jnp.float32), pieces)
    pieces = jnp.where(lane == 2, low, pieces)
    own_ref[:, :D] = tgt
    own_ref[:, D:] = pieces.astype(jnp.bfloat16)


def pack(targets, potential, logw):
    return pl.pallas_call(
        pack_kernel,
        grid=(1,),
        in_specs=[whole(OWN, D), whole(1, OWN), whole(1, OWN)],
        out_specs=[whole(OWN, D + PAD), whole(1, OWN)],
        out_shape=[
            jax.ShapeDtypeStruct((OWN, D + PAD), jnp.bfloat16),
            jax.ShapeDtypeStruct((1, OWN), jnp.float32),
        ],
        compiler_params=pltpu.CompilerParams(vmem_limit_bytes=VMEM),
        name="pack",
    )(targets, potential.reshape(1, OWN), logw.reshape(1, OWN))


def score_rows(group_refs, src_ref, cross_ref, lse_ref, kept_ref, sems):
    group = jnp.concatenate([ref[...] for ref in group_refs], axis=0)
    pieces = group[:, D:].astype(jnp.float32)
    bias = pieces[:, 0:1] + pieces[:, 1:2] + pieces[:, 2:3]
    group = group[:, :D]
    copies = []
    for at in range(PARTS):
        part = slice(at * BLOCK, (at + 1) * BLOCK)
        cross = SCALE * lax.dot_general(
            group,
            src_ref[part, :],
            (((1,), (1,)), ((), ())),
            preferred_element_type=jnp.float32,
        )
        cross_ref[:, part] = cross
        if kept_ref is not None:
            copy = pltpu.make_async_copy(cross_ref.at[:, part], kept_ref.at[:, part], sems.at[at])
            copy.start()
            copies.append(copy)
        lse_ref[:, part] = log_sum2(cross + bias)
    return copies


def row_pass(groups, sources):
    count = len(groups)
    rows = sum(group.shape[0] for group in groups)

    def body(*refs):
        group_refs, (src_ref, kept_ref, lse_ref, cross_ref, sems) = refs[:count], refs[count:]
        for copy in score_rows(group_refs, src_ref, cross_ref, lse_ref, kept_ref, sems):
            copy.wait()

    return pl.pallas_call(
        body,
        in_specs=[IN_VMEM] * (count + 1),
        out_specs=[IN_HBM, IN_VMEM],
        out_shape=[
            pltpu.HBM((rows, HALF), jnp.float32),
            jax.ShapeDtypeStruct((1, HALF), jnp.float32),
        ],
        scratch_shapes=[
            pltpu.VMEM((rows, HALF), jnp.float32),
            pltpu.SemaphoreType.DMA((PARTS,)),
        ],
        compiler_params=pltpu.CompilerParams(vmem_limit_bytes=VMEM),
        cost_estimate=pl.CostEstimate(
            flops=2 * rows * HALF * D,
            bytes_accessed=HALF * D * 2 + rows * HALF * 4,
            transcendentals=rows * HALF,
        ),
        name="rows",
    )(*groups, sources)


def last_kernel(count, earlier_count, *refs):
    x_ref, refs = refs[0], refs[1:]
    group_refs, (src_ref, faced_ref, logw_ref) = refs[:count], refs[count : count + 3]
    refs = refs[count + 3 :]
    earlier, refs = refs[:earlier_count], refs[earlier_count:]
    kept_ref, far_kept_ref, near_ref, lse_ref, cross_ref, far_ref, own_row, faced_row, sems = refs
    copies = score_rows(group_refs[-1:], src_ref, cross_ref, own_row, kept_ref, sems.at[0])
    top = 0
    for at in range(0, count, 2):
        groups = group_refs[at : at + 2]
        rows = sum(ref.shape[0] for ref in groups)
        faced_part = faced_row.at[at // 2 : at // 2 + 1, :]
        if top < NEAR:
            held = near_ref.at[top : top + rows, :]
            score_rows(groups, faced_ref, held, faced_part, None, None)
        else:
            here = slice(top - NEAR, top - NEAR + rows)
            copies += score_rows(
                groups,
                faced_ref,
                far_ref.at[here, :],
                faced_part,
                far_kept_ref.at[here, :],
                sems.at[1 + at // 2],
            )
        top += rows
    own = log_sum2(jnp.concatenate([own_row[...], *[ref[...] for ref in earlier]], axis=0))
    faced = log_sum2(faced_row[...])
    mine = pl.multiple_of(x_ref[0] * HALF, HALF)
    other = pl.multiple_of((1 - x_ref[0]) * HALF, HALF)
    logw = logw_ref[...]
    for peer in range(PEERS):
        lse_ref[peer, :, pl.ds(mine, HALF)] = own
        lse_ref[peer, :, pl.ds(other, HALF)] = faced
        lse_ref[peer, :, 2 * HALF :] = logw
    for copy in copies:
        copy.wait()


def last_pass(x_hi, groups, sources, faced, logw, earlier):
    count = len(groups)
    rows = groups[-1].shape[0]
    passes = (count + 1) // 2

    def body(*refs):
        last_kernel(count, len(earlier), *refs)

    return pl.pallas_call(
        body,
        in_specs=[IN_SMEM] + [IN_VMEM] * (count + 3 + len(earlier)),
        out_specs=[IN_HBM, IN_HBM, IN_VMEM, IN_VMEM],
        out_shape=[
            pltpu.HBM((rows, HALF), jnp.float32),
            pltpu.HBM((ROWS - NEAR, HALF), jnp.float32),
            pltpu.VMEM((NEAR, HALF), jnp.float32),
            pltpu.VMEM((PEERS, 1, 3 * HALF), jnp.float32),
        ],
        scratch_shapes=[
            pltpu.VMEM((rows, HALF), jnp.float32),
            pltpu.VMEM((ROWS - NEAR, HALF), jnp.float32),
            pltpu.VMEM((1, HALF), jnp.float32),
            pltpu.VMEM((passes, HALF), jnp.float32),
            pltpu.SemaphoreType.DMA((1 + passes, PARTS)),
        ],
        compiler_params=pltpu.CompilerParams(vmem_limit_bytes=VMEM),
        cost_estimate=pl.CostEstimate(
            flops=2 * (rows + ROWS) * HALF * D,
            bytes_accessed=HALF * D * 2 + (rows + ROWS) * HALF * 4,
            transcendentals=(rows + ROWS) * HALF,
        ),
        name="last_rows",
    )(x_hi, *groups, sources, faced, logw, *earlier)


def column_kernel(place_ref, *refs):
    own_refs, refs = refs[:STEPS], refs[STEPS:]
    far_ref, near_ref, partial_ref, sq_ref, out_ref, pot_ref, own_held, far_held, sems = refs
    copies, top = [], 0
    for own_ref in own_refs:
        for at in range(0, own_ref.shape[0], UNIT):
            here = slice(top, top + UNIT)
            unit = len(copies)
            fetches = [
                pltpu.make_async_copy(
                    own_ref.at[at : at + UNIT, :], own_held.at[here, :], sems.at[0, unit]
                )
            ]
            if top >= NEAR:
                here = slice(top - NEAR, top - NEAR + UNIT)
                fetches.append(
                    pltpu.make_async_copy(
                        far_ref.at[here, :], far_held.at[here, :], sems.at[1, unit]
                    )
                )
            for fetch in fetches:
                fetch.start()
            copies.append(fetches)
            top += UNIT
    x_hi, z, core = place_ref[0], place_ref[1], place_ref[2]
    mine = pl.multiple_of(x_hi * HALF, HALF)
    other = pl.multiple_of((1 - x_hi) * HALF, HALF)

    def bias(start, peer):
        row = log_sum2(partial_ref[:, 0, pl.ds(start, HALF)])
        logw = partial_ref[pl.ds(peer, 1), 0, 2 * HALF :]
        return row, jnp.broadcast_to(logw * LOG2E - row, (8, HALF))

    row, own_bias = bias(mine, x_hi)
    _, faced_bias = bias(other, 1 - x_hi)
    pot_ref[...] = sq_ref[...] - BACK * row
    side = 2 * core - 1
    top = 0
    for step, own_ref in enumerate(own_refs):
        for at in range(0, own_ref.shape[0], UNIT):
            peaks, totals = [], []
            for copy in copies[top // UNIT]:
                copy.wait()
            for row_at in range(top, top + UNIT, 8):
                scores = own_held[row_at : row_at + 8, :] + own_bias
                pieces = [scores[:, k : k + LANES] for k in range(0, HALF, LANES)]
                if top < NEAR:
                    scores = near_ref[row_at : row_at + 8, :] + faced_bias
                else:
                    scores = far_held[row_at - NEAR : row_at - NEAR + 8, :] + faced_bias
                pieces += [scores[:, k : k + LANES] for k in range(0, HALF, LANES)]
                peak = pieces[0]
                for piece in pieces[1:]:
                    peak = jnp.maximum(peak, piece)
                total = jnp.exp2(pieces[0] - peak)
                for piece in pieces[1:]:
                    total = total + jnp.exp2(piece - peak)
                peaks.append(peak)
                totals.append(total)
            peak = jnp.concatenate(peaks, axis=0).T
            total = jnp.concatenate(totals, axis=0).T
            highest = jnp.max(peak, axis=0, keepdims=True)
            total = jnp.sum(total * jnp.exp2(peak - highest), axis=0, keepdims=True)
            lse = highest + jnp.log2(total)
            top += UNIT
            if step == 0:
                first, second = 2 * z + core, 2 * z + 1 - core
            else:
                chip = lax.rem(z + UNITS + (side if at == 0 else -side) * step, UNITS)
                first, second = 2 * chip, 2 * chip + 1
            out_ref[pl.ds(first, 1)] = lse[:, :OWN].reshape(1, 1, OWN)
            out_ref[pl.ds(second, 1)] = lse[:, OWN:].reshape(1, 1, OWN)


def column_pass(place, own_crosses, far, near, partial, src_sq):
    return pl.pallas_call(
        column_kernel,
        in_specs=[IN_SMEM] + [IN_HBM] * (STEPS + 1) + [IN_VMEM] * 3,
        out_specs=[IN_VMEM] * 2,
        out_shape=[
            jax.ShapeDtypeStruct((PEERS, 1, OWN), jnp.float32),
            jax.ShapeDtypeStruct((1, HALF), jnp.float32),
        ],
        scratch_shapes=[
            pltpu.VMEM((ROWS, HALF), jnp.float32),
            pltpu.VMEM((ROWS - NEAR, HALF), jnp.float32),
            pltpu.SemaphoreType.DMA((2, UNITS)),
        ],
        compiler_params=pltpu.CompilerParams(vmem_limit_bytes=VMEM),
        cost_estimate=pl.CostEstimate(
            flops=12 * ROWS * HALF, bytes_accessed=ROWS * HALF * 8, transcendentals=2 * ROWS * HALF
        ),
        name="columns",
    )(
        place,
        *[pltpu.with_memory_space_constraint(cross, pltpu.HBM) for cross in (*own_crosses, far)],
        pltpu.with_memory_space_constraint(near, pltpu.VMEM),
        partial,
        src_sq,
    )


def on_device(sources, targets, potential_in, source_logw, target_logw):
    place = jnp.stack([lax.axis_index(axis) for axis in ("x_hi", "z", "core")]).astype(jnp.int32)
    faced_sources = facing(sources)
    own, tgt_sq = pack(targets, potential_in, target_logw)
    same, cross_core = onward(own), onward_across(own)
    beside = other_core(own)

    src_sq = jnp.sum(jnp.square(sources.astype(jnp.float32)), axis=1)
    first = lax.axis_index("core") == 0
    unit = jnp.concatenate(
        [jnp.where(first, same, cross_core), jnp.where(first, cross_core, same)], axis=0
    )
    groups, crosses, lses = [], [], []
    pending = [own, beside]
    for step in (1, 2, 3):
        following = onward(unit)
        beside = other_core(unit)
        cross, lse = row_pass(pending, sources)
        groups += pending
        crosses.append(cross)
        lses.append(lse)
        following, lses[-1], src_sq = lax.optimization_barrier((following, lses[-1], src_sq))
        pending = [unit, beside]
        unit = following
    cross, lse = row_pass(pending, sources)
    groups += [*pending, unit]
    crosses.append(cross)
    lses.append(lse)
    cross, far, near, shared = last_pass(
        place, groups, sources, faced_sources, source_logw.reshape(1, HALF), lses
    )
    crosses.append(cross)

    partial = lax.all_to_all(shared, ("y", "x_lo", "x_hi"), 0, 0, tiled=True)
    columns, source_potential = column_pass(
        place, crosses, far, near, partial, src_sq.reshape(1, HALF)
    )
    gathered = lax.all_to_all(columns, ("z", "core"), 0, 0, tiled=True)
    final = log_sum2(gathered.reshape(PEERS, OWN)).reshape(OWN)
    potential_out = tgt_sq.reshape(OWN) - BACK * final
    return (source_potential.reshape(HALF), potential_out)


def solution(mesh):
    every = ("y", "x_lo", "z", "x_hi", "core")
    blk = ("z", "x_hi", "core")
    fine = Mesh(mesh.devices.reshape(4, 2, 8, 2, 2), every)
    in_specs = (P(blk, None), P(every, None), P(every), P(blk), P(every))
    out_specs = (P(blk), P(every))
    return jax.shard_map(
        on_device, mesh=fine, in_specs=in_specs, out_specs=out_specs, check_vma=False
    )
```

```python
import math

import jax
import jax.numpy as jnp
from jax import lax
from jax.experimental import pallas as pl
from jax.experimental.pallas import tpu as pltpu
from jax.sharding import Mesh, PartitionSpec as P

EPSILON = 0.05
LOG2E = math.log2(math.e)
SCALE = 2.0 / EPSILON * LOG2E
BACK = EPSILON * math.log(2.0)

D = 768
PAD = 128
OWN = 64
UNIT = 2 * OWN
UNITS = 8
ROWS = UNIT * UNITS
HALF = 1024
BLOCK = 512
LANES = 128
PEERS = 16
X_HI, Z, CORE, ODD = range(4)
STEPS = 5
VMEM = 12 * 1024 * 1024
EDGE = HALF // 4
EXTRA = 16
REST = ROWS - UNIT
IN_VMEM = pl.BlockSpec(memory_space=pltpu.VMEM)
IN_HBM = pl.BlockSpec(memory_space=pl.ANY)
IN_SMEM = pl.BlockSpec(memory_space=pltpu.SMEM)


def whole(*shape):
    return pl.BlockSpec(shape, lambda i: (0,) * len(shape))


def onward(value):
    count = lax.axis_size("z")
    up = [(2 * i, 2 * ((i + 1) % count)) for i in range(count)]
    down = [(2 * i + 1, 2 * ((i - 1) % count) + 1) for i in range(count)]
    return lax.ppermute(value, ("z", "core"), up + down)


def onward_across(value):
    count = lax.axis_size("z")
    up = [(2 * i + 1, 2 * ((i + 1) % count)) for i in range(count)]
    down = [(2 * i, 2 * ((i - 1) % count) + 1) for i in range(count)]
    return lax.ppermute(value, ("z", "core"), up + down)


def other_core(value):
    return lax.ppermute(value, "core", [(0, 1), (1, 0)])


def facing(value):
    return lax.ppermute(value, ("x_lo", "x_hi"), [(0, 3), (3, 0), (1, 2), (2, 1)])


def beside_y(value):
    return lax.ppermute(value, "y", [(0, 1), (1, 0), (2, 3), (3, 2)])


def log_sum2(values):
    peak = jnp.max(values, axis=0, keepdims=True)
    return peak + jnp.log2(jnp.sum(jnp.exp2(values - peak), axis=0, keepdims=True))


def split(values):
    high = values.astype(jnp.bfloat16).astype(jnp.float32)
    rest = values - high
    middle = rest.astype(jnp.bfloat16).astype(jnp.float32)
    return high, middle, rest - middle


def pack_kernel(place_ref, src_hbm, tgt_hbm, pot_hbm, logw_hbm, *refs):
    src_logw_hbm, own_ref, sq_ref, edge_ref, tgt_ref, pot_ref, logw_ref, src_logw_ref, sems = refs
    copies = [
        pltpu.make_async_copy(source, target, sems.at[at])
        for at, (source, target) in enumerate(
            (
                (tgt_hbm, tgt_ref),
                (pot_hbm, pot_ref),
                (logw_hbm, logw_ref),
                (src_logw_hbm, src_logw_ref),
            )
        )
    ]
    for copy in copies:
        copy.start()
    start = pl.multiple_of(place_ref[ODD] * (HALF - EDGE), EDGE)
    edge = pltpu.make_async_copy(
        src_hbm.at[pl.ds(start, EDGE), :], edge_ref.at[:EDGE, :], sems.at[4]
    )
    edge.start()
    for copy in copies:
        copy.wait()
    tgt = tgt_ref[...]
    wide = tgt.astype(jnp.float32)
    sq = jnp.sum(wide * wide, axis=1, keepdims=True)
    diagonal = lax.broadcasted_iota(jnp.int32, (OWN, OWN), 0) == lax.broadcasted_iota(
        jnp.int32, (OWN, OWN), 1
    )

    def upright(row):
        return jnp.sum(jnp.where(diagonal, row, 0.0), axis=1, keepdims=True)

    sq_ref[...] = jnp.sum(jnp.where(diagonal, sq, 0.0), axis=0, keepdims=True)
    bias = (upright(logw_ref[...]) + (upright(pot_ref[...]) - sq) / EPSILON) * LOG2E
    high, middle, low = split(bias)
    lane = lax.broadcasted_iota(jnp.int32, (OWN, PAD), 1)
    pieces = jnp.where(lane == 0, high, 0.0)
    pieces = jnp.where(lane == 1, middle, pieces)
    pieces = jnp.where(lane == 2, low, pieces)
    own_ref[:, :D] = tgt
    own_ref[:, D:] = pieces.astype(jnp.bfloat16)
    line = lax.broadcasted_iota(jnp.int32, (EXTRA, D), 0)
    extra = jnp.zeros((EXTRA, D), jnp.float32)
    for quarter in range(HALF // EDGE):
        part = src_logw_ref[:, quarter * EDGE : (quarter + 1) * EDGE]
        row = jnp.concatenate(split(part), axis=1)
        extra = jnp.where(line == quarter, row, extra)
    edge_ref[EDGE:, :] = extra.astype(jnp.bfloat16)
    edge.wait()


def in_hbm(*values):
    return [pltpu.with_memory_space_constraint(value, pltpu.HBM) for value in values]


def pack(place, sources, targets, potential, logw, src_logw):
    return pl.pallas_call(
        pack_kernel,
        in_specs=[IN_SMEM] + [IN_HBM] * 5,
        out_specs=[IN_VMEM] * 3,
        out_shape=[
            jax.ShapeDtypeStruct((OWN, D + PAD), jnp.bfloat16),
            jax.ShapeDtypeStruct((1, OWN), jnp.float32),
            jax.ShapeDtypeStruct((EDGE + EXTRA, D), jnp.bfloat16),
        ],
        scratch_shapes=[
            pltpu.VMEM((OWN, D), jnp.bfloat16),
            pltpu.VMEM((1, OWN), jnp.float32),
            pltpu.VMEM((1, OWN), jnp.float32),
            pltpu.VMEM((1, HALF), jnp.float32),
            pltpu.SemaphoreType.DMA((5,)),
        ],
        compiler_params=pltpu.CompilerParams(vmem_limit_bytes=VMEM),
        name="pack",
    )(
        place,
        *in_hbm(
            sources,
            targets,
            potential.reshape(1, OWN),
            logw.reshape(1, OWN),
            src_logw.reshape(1, HALF),
        ),
    )


def score_rows(group_refs, src_refs, cross_ref, lse_ref):
    group = jnp.concatenate([ref[...] for ref in group_refs], axis=0)
    pieces = group[:, D:].astype(jnp.float32)
    bias = pieces[:, 0:1] + pieces[:, 1:2] + pieces[:, 2:3]
    group = group[:, :D]
    place = 0
    for src_ref in src_refs:
        height = src_ref.shape[0] // EDGE * EDGE
        rows = min(BLOCK, height)
        for start in range(0, height, rows):
            cross = SCALE * lax.dot_general(
                group,
                src_ref[start : start + rows, :],
                (((1,), (1,)), ((), ())),
                preferred_element_type=jnp.float32,
            )
            cross_ref[:, place : place + rows] = cross
            lse_ref[:, place : place + rows] = log_sum2(cross + bias)
            place += rows


def row_pass(groups, sources):
    count, parts = len(groups), len(sources)
    small = 2 if parts > 1 else 1
    rows = sum(group.shape[0] for group in groups)
    passes = (count + 1) // 2

    def body(*refs):
        group_refs, src_refs, refs = (
            refs[:count],
            refs[count : count + parts],
            refs[count + parts :],
        )
        kept_ref, lse_ref, *logw_refs, cross_ref, row_ref, sems = refs
        for logw_ref in logw_refs:
            extra = src_refs[0][EDGE:, :].astype(jnp.float32)
            sums = extra[:, :EDGE] + extra[:, EDGE : 2 * EDGE] + extra[:, 2 * EDGE :]
            for quarter in range(HALF // EDGE):
                here = slice(quarter * EDGE, (quarter + 1) * EDGE)
                logw_ref[:, here] = sums[quarter : quarter + 1, :]
        copies, top = [], 0
        for at in range(passes):
            pair = group_refs[2 * at : 2 * at + 2]
            here = slice(top, top + sum(ref.shape[0] for ref in pair))
            score_rows(pair, src_refs, cross_ref.at[here, :], row_ref.at[at : at + 1, :])
            copies.append(
                pltpu.make_async_copy(cross_ref.at[here, :], kept_ref.at[here, :], sems.at[at])
            )
            copies[-1].start()
            top = here.stop
        lse_ref[...] = log_sum2(row_ref[...])
        for copy in copies:
            copy.wait()

    return pl.pallas_call(
        body,
        in_specs=[IN_VMEM] * (count + parts),
        out_specs=[IN_HBM] + [IN_VMEM] * small,
        out_shape=[pltpu.HBM((rows, HALF), jnp.float32)]
        + [jax.ShapeDtypeStruct((1, HALF), jnp.float32)] * small,
        scratch_shapes=[
            pltpu.VMEM((rows, HALF), jnp.float32),
            pltpu.VMEM((passes, HALF), jnp.float32),
            pltpu.SemaphoreType.DMA((passes,)),
        ],
        compiler_params=pltpu.CompilerParams(vmem_limit_bytes=VMEM),
        cost_estimate=pl.CostEstimate(flops=1, bytes_accessed=1, transcendentals=0),
        name="rows",
    )(*groups, *sources)


def edge_places(place_ref):
    straight = pl.multiple_of(place_ref[ODD] * (HALF - EDGE), EDGE)
    return straight, pl.multiple_of((1 - place_ref[ODD]) * (HALF - EDGE), EDGE)


def last_kernel(place_ref, group_ref, *refs):
    own_refs, faced_refs, (faced_earlier, *earlier), refs = (
        refs[:1],
        refs[1:4],
        refs[4 : 4 + STEPS],
        refs[4 + STEPS :],
    )
    cross_ref, lse_ref, own_row, faced_row = refs
    score_rows([group_ref], own_refs, cross_ref.at[:, :HALF], own_row)
    score_rows([group_ref], faced_refs, cross_ref.at[:, HALF:], faced_row)
    own = log_sum2(jnp.concatenate([own_row[...], *[ref[...] for ref in earlier]], axis=0))
    faced = log_sum2(jnp.concatenate([faced_row[...], faced_earlier[...]], axis=0))
    mine = pl.multiple_of(place_ref[X_HI] * HALF, HALF)
    other = pl.multiple_of((1 - place_ref[X_HI]) * HALF, HALF)
    straight, around = edge_places(place_ref)
    for peer in range(PEERS):
        lse_ref[peer, :, pl.ds(mine, HALF)] = own
        lse_ref[peer, :, pl.ds(other + straight, EDGE)] = faced[:, :EDGE]
        lse_ref[peer, :, pl.ds(other + EDGE, HALF - 2 * EDGE)] = faced[:, EDGE : HALF - EDGE]
        lse_ref[peer, :, pl.ds(other + around, EDGE)] = faced[:, HALF - EDGE :]


def last_pass(place, group, sources, faced, faced_earlier, earlier):
    work = 2 * UNIT * HALF
    return pl.pallas_call(
        last_kernel,
        in_specs=[IN_SMEM] + [IN_VMEM] * (6 + len(earlier)),
        out_specs=[IN_VMEM] * 2,
        out_shape=[
            pltpu.VMEM((UNIT, 2 * HALF), jnp.float32),
            pltpu.VMEM((PEERS, 1, 2 * HALF), jnp.float32),
        ],
        scratch_shapes=[
            pltpu.VMEM((1, HALF), jnp.float32),
            pltpu.VMEM((1, HALF), jnp.float32),
        ],
        compiler_params=pltpu.CompilerParams(vmem_limit_bytes=VMEM),
        cost_estimate=pl.CostEstimate(
            flops=2 * work * D, bytes_accessed=HALF * D * 4 + work * 4, transcendentals=work
        ),
        name="last_rows",
    )(place, group, sources, *faced, faced_earlier, *earlier)


def column_kernel(heights, place_ref, *refs):
    own_kept, refs = refs[: len(heights)], refs[len(heights) :]
    faced_kept, near_ref, partial_ref, sq_ref, logw_ref, faced_logw_ref = refs[:6]
    out_ref, pot_ref, own_held, faced_held, sems = refs[6:]
    copies, top = [], 0
    for height, own_ref in zip(heights, own_kept):
        for start in range(0, height, UNIT):
            here = slice(top, top + UNIT)
            at = len(copies)
            copies.append(
                (
                    pltpu.make_async_copy(
                        own_ref.at[start : start + UNIT, :], own_held.at[here, :], sems.at[0, at]
                    ),
                    pltpu.make_async_copy(
                        faced_kept.at[here, :], faced_held.at[here, :], sems.at[1, at]
                    ),
                )
            )
            top += UNIT
    for pair in copies:
        for copy in pair:
            copy.start()
    z, core = place_ref[Z], place_ref[CORE]
    mine = pl.multiple_of(place_ref[X_HI] * HALF, HALF)
    other = pl.multiple_of((1 - place_ref[X_HI]) * HALF, HALF)
    straight, around = edge_places(place_ref)

    row = log_sum2(partial_ref[:, 0, pl.ds(mine, HALF)])
    own_bias = logw_ref[...] * LOG2E - row
    pot_ref[...] = sq_ref[...] - BACK * row
    own_bias = jnp.broadcast_to(own_bias, (8, HALF))
    faced_bias = [
        faced_logw_ref[:, pl.ds(start, width)] * LOG2E
        - log_sum2(partial_ref[:, 0, pl.ds(other + start, width)])
        for start, width in ((straight, EDGE), (EDGE, HALF - 2 * EDGE), (around, EDGE))
    ]
    faced_bias = jnp.broadcast_to(jnp.concatenate(faced_bias, axis=1), (8, HALF))
    side = 2 * core - 1
    for unit in (UNITS - 1, *range(UNITS - 1)):
        if unit < len(copies):
            for copy in copies[unit]:
                copy.wait()
            own_ref, faced_ref, top = own_held, faced_held, unit * UNIT
        else:
            own_ref, faced_ref, top = near_ref.at[:, :HALF], near_ref.at[:, HALF:], 0
        peaks, totals = [], []
        for at in range(top, top + UNIT, 8):
            pieces = []
            for ref, added in ((own_ref, own_bias), (faced_ref, faced_bias)):
                scores = ref[at : at + 8, :] + added
                pieces += [scores[:, k : k + LANES] for k in range(0, HALF, LANES)]
            peak = pieces[0]
            for piece in pieces[1:]:
                peak = jnp.maximum(peak, piece)
            total = jnp.exp2(pieces[0] - peak)
            for piece in pieces[1:]:
                total = total + jnp.exp2(piece - peak)
            peaks.append(peak)
            totals.append(total)
        peak = jnp.concatenate(peaks, axis=0).T
        total = jnp.concatenate(totals, axis=0).T
        highest = jnp.max(peak, axis=0, keepdims=True)
        total = jnp.sum(total * jnp.exp2(peak - highest), axis=0, keepdims=True)
        lse = highest + jnp.log2(total)
        if unit == 0:
            first, second = 2 * z + core, 2 * z + 1 - core
        else:
            step = (unit + 1) // 2
            chip = lax.rem(z + UNITS + (side if unit % 2 else -side) * step, UNITS)
            first, second = 2 * chip, 2 * chip + 1
        out_ref[pl.ds(first, 1)] = lse[:, :OWN].reshape(1, 1, OWN)
        out_ref[pl.ds(second, 1)] = lse[:, OWN:].reshape(1, 1, OWN)


def column_pass(place, own_crosses, faced_cross, near, partial, *rows):
    heights = [cross.shape[0] for cross in own_crosses]

    def body(*refs):
        column_kernel(heights, *refs)

    return pl.pallas_call(
        body,
        in_specs=[IN_SMEM] + [IN_HBM] * (len(own_crosses) + 1) + [IN_VMEM] * 5,
        out_specs=[IN_VMEM] * 2,
        out_shape=[
            jax.ShapeDtypeStruct((PEERS, 1, OWN), jnp.float32),
            jax.ShapeDtypeStruct((1, HALF), jnp.float32),
        ],
        scratch_shapes=[
            pltpu.VMEM((REST, HALF), jnp.float32),
            pltpu.VMEM((REST, HALF), jnp.float32),
            pltpu.SemaphoreType.DMA((2, UNITS - 1)),
        ],
        compiler_params=pltpu.CompilerParams(vmem_limit_bytes=VMEM),
        cost_estimate=pl.CostEstimate(
            flops=12 * ROWS * HALF, bytes_accessed=ROWS * HALF * 8, transcendentals=2 * ROWS * HALF
        ),
        name="columns",
    )(
        place,
        *in_hbm(*own_crosses, faced_cross),
        pltpu.with_memory_space_constraint(near, pltpu.VMEM),
        partial,
        *[row.reshape(1, HALF) for row in rows],
    )


def on_device(sources, targets, potential_in, source_logw, target_logw):
    place = jnp.stack(
        [
            lax.axis_index("x_hi"),
            lax.axis_index("z"),
            lax.axis_index("core"),
            lax.axis_index("y") % 2,
        ]
    ).astype(jnp.int32)
    own, tgt_sq, edge = pack(
        place, sources, targets, potential_in, target_logw, source_logw
    )
    straight = facing(edge)
    same, cross_core = onward(own), onward_across(own)
    middle = facing(sources[EDGE : HALF - EDGE])
    beside = other_core(own)

    first = lax.axis_index("core") == 0
    unit = jnp.concatenate(
        [jnp.where(first, same, cross_core), jnp.where(first, cross_core, same)], axis=0
    )
    src_sq = jnp.sum(jnp.square(sources.astype(jnp.float32)), axis=1)
    groups, crosses, lses = [], [], []
    pending = [own, beside]
    for step in (1, 2, 3):
        following = onward(unit)
        beside = other_core(unit)
        if step == 1:
            around = beside_y(straight)
        cross, lse = row_pass(pending, [sources])
        groups += pending
        crosses.append(cross)
        if step == 1:
            following, lse, src_sq = lax.optimization_barrier((following, lse, src_sq))
        else:
            following, lse = lax.optimization_barrier((following, lse))
        lses.append(lse)
        pending = [unit, beside]
        unit = following
    cross, lse = row_pass(pending, [sources])
    groups += pending
    crosses.append(cross)
    faced = [straight, middle, around]
    faced_cross, faced_lse, faced_logw = row_pass(groups, faced)
    unit, lse, faced_lse = lax.optimization_barrier((unit, lse, faced_lse))
    lses.append(lse)
    near, shared = last_pass(place, unit, sources, faced, faced_lse, lses)

    partial = lax.all_to_all(shared, ("y", "x_lo", "x_hi"), 0, 0, tiled=True)
    columns, source_potential = column_pass(
        place, crosses, faced_cross, near, partial, src_sq, source_logw, faced_logw
    )
    gathered = lax.all_to_all(columns, ("z", "core"), 0, 0, tiled=True)
    final = log_sum2(gathered.reshape(PEERS, OWN)).reshape(OWN)
    potential_out = tgt_sq.reshape(OWN) - BACK * final
    return (source_potential.reshape(HALF), potential_out)


def solution(mesh):
    every = ("y", "x_lo", "z", "x_hi", "core")
    blk = ("z", "x_hi", "core")
    fine = Mesh(mesh.devices.reshape(4, 2, 8, 2, 2), every)
    in_specs = (P(blk, None), P(every, None), P(every), P(blk), P(every))
    out_specs = (P(blk), P(every))
    return jax.shard_map(
        on_device, mesh=fine, in_specs=in_specs, out_specs=out_specs, check_vma=False
    )
```

```python
import math

import jax
import jax.numpy as jnp
from jax import lax
from jax.experimental import pallas as pl
from jax.experimental.pallas import tpu as pltpu
from jax.sharding import Mesh, PartitionSpec as P

EPSILON = 0.05
LOG2E = math.log2(math.e)
SCALE = 2.0 / EPSILON * LOG2E
BACK = EPSILON * math.log(2.0)

D = 768
PAD = 128
OWN = 64
UNIT = 2 * OWN
UNITS = 8
ROWS = UNIT * UNITS
HALF = 1024
BLOCK = 512
LANES = 128
PEERS = 16
X_HI, Z, CORE, QUARTERS, SENT = 0, 1, 2, 3, 7
PART = HALF // 2
STEPS = 5
VMEM = 12 * 1024 * 1024
EDGE = HALF // 4
EXTRA = 16
REST = ROWS - UNIT
IN_VMEM = pl.BlockSpec(memory_space=pltpu.VMEM)
IN_HBM = pl.BlockSpec(memory_space=pl.ANY)
IN_SMEM = pl.BlockSpec(memory_space=pltpu.SMEM)


def whole(*shape):
    return pl.BlockSpec(shape, lambda i: (0,) * len(shape))


def onward(value):
    count = lax.axis_size("z")
    up = [(2 * i, 2 * ((i + 1) % count)) for i in range(count)]
    down = [(2 * i + 1, 2 * ((i - 1) % count) + 1) for i in range(count)]
    return lax.ppermute(value, ("z", "core"), up + down)


def onward_across(value):
    count = lax.axis_size("z")
    up = [(2 * i + 1, 2 * ((i + 1) % count)) for i in range(count)]
    down = [(2 * i, 2 * ((i - 1) % count) + 1) for i in range(count)]
    return lax.ppermute(value, ("z", "core"), up + down)


def other_core(value):
    return lax.ppermute(value, "core", [(0, 1), (1, 0)])


def facing(value):
    return lax.ppermute(value, ("x_lo", "x_hi"), [(0, 3), (3, 0), (1, 2), (2, 1)])


def beside_x(value):
    return lax.ppermute(value, "x_lo", [(0, 1), (1, 0)])


def beside_y(value):
    return lax.ppermute(value, "y", [(0, 1), (1, 0), (2, 3), (3, 2)])


def log_sum2(values):
    peak = jnp.max(values, axis=0, keepdims=True)
    return peak + jnp.log2(jnp.sum(jnp.exp2(values - peak), axis=0, keepdims=True))


def split(values):
    high = values.astype(jnp.bfloat16).astype(jnp.float32)
    rest = values - high
    middle = rest.astype(jnp.bfloat16).astype(jnp.float32)
    return high, middle, rest - middle


def pack_kernel(place_ref, src_hbm, tgt_hbm, pot_hbm, logw_hbm, *refs):
    src_logw_hbm, own_ref, sq_ref, edge_ref, tgt_ref, pot_ref, logw_ref, src_logw_ref, sems = refs
    copies = [
        pltpu.make_async_copy(source, target, sems.at[at])
        for at, (source, target) in enumerate(
            (
                (tgt_hbm, tgt_ref),
                (pot_hbm, pot_ref),
                (logw_hbm, logw_ref),
                (src_logw_hbm, src_logw_ref),
            )
        )
    ]
    for copy in copies:
        copy.start()
    start = pl.multiple_of(place_ref[SENT] * EDGE, EDGE)
    edge = pltpu.make_async_copy(
        src_hbm.at[pl.ds(start, EDGE), :], edge_ref.at[:EDGE, :], sems.at[4]
    )
    edge.start()
    for copy in copies:
        copy.wait()
    tgt = tgt_ref[...]
    wide = tgt.astype(jnp.float32)
    sq = jnp.sum(wide * wide, axis=1, keepdims=True)
    diagonal = lax.broadcasted_iota(jnp.int32, (OWN, OWN), 0) == lax.broadcasted_iota(
        jnp.int32, (OWN, OWN), 1
    )

    def upright(row):
        return jnp.sum(jnp.where(diagonal, row, 0.0), axis=1, keepdims=True)

    sq_ref[...] = jnp.sum(jnp.where(diagonal, sq, 0.0), axis=0, keepdims=True)
    bias = (upright(logw_ref[...]) + (upright(pot_ref[...]) - sq) / EPSILON) * LOG2E
    high, middle, low = split(bias)
    lane = lax.broadcasted_iota(jnp.int32, (OWN, PAD), 1)
    pieces = jnp.where(lane == 0, high, 0.0)
    pieces = jnp.where(lane == 1, middle, pieces)
    pieces = jnp.where(lane == 2, low, pieces)
    own_ref[:, :D] = tgt
    own_ref[:, D:] = pieces.astype(jnp.bfloat16)
    line = lax.broadcasted_iota(jnp.int32, (EXTRA, D), 0)
    extra = jnp.zeros((EXTRA, D), jnp.float32)
    for quarter in range(HALF // EDGE):
        part = src_logw_ref[:, quarter * EDGE : (quarter + 1) * EDGE]
        row = jnp.concatenate(split(part), axis=1)
        extra = jnp.where(line == quarter, row, extra)
    edge_ref[EDGE:, :] = extra.astype(jnp.bfloat16)
    edge.wait()


def in_hbm(*values):
    return [pltpu.with_memory_space_constraint(value, pltpu.HBM) for value in values]


def pack(place, sources, targets, potential, logw, src_logw):
    return pl.pallas_call(
        pack_kernel,
        in_specs=[IN_SMEM] + [IN_HBM] * 5,
        out_specs=[IN_VMEM] * 3,
        out_shape=[
            jax.ShapeDtypeStruct((OWN, D + PAD), jnp.bfloat16),
            jax.ShapeDtypeStruct((1, OWN), jnp.float32),
            jax.ShapeDtypeStruct((EDGE + EXTRA, D), jnp.bfloat16),
        ],
        scratch_shapes=[
            pltpu.VMEM((OWN, D), jnp.bfloat16),
            pltpu.VMEM((1, OWN), jnp.float32),
            pltpu.VMEM((1, OWN), jnp.float32),
            pltpu.VMEM((1, HALF), jnp.float32),
            pltpu.SemaphoreType.DMA((5,)),
        ],
        compiler_params=pltpu.CompilerParams(vmem_limit_bytes=VMEM),
        name="pack",
    )(
        place,
        *in_hbm(
            sources,
            targets,
            potential.reshape(1, OWN),
            logw.reshape(1, OWN),
            src_logw.reshape(1, HALF),
        ),
    )


def score_rows(group_refs, src_refs, cross_ref, lse_ref):
    group = jnp.concatenate([ref[...] for ref in group_refs], axis=0)
    pieces = group[:, D:].astype(jnp.float32)
    bias = pieces[:, 0:1] + pieces[:, 1:2] + pieces[:, 2:3]
    group = group[:, :D]
    place = 0
    for src_ref in src_refs:
        height = src_ref.shape[0] // EDGE * EDGE
        rows = min(BLOCK, height)
        for start in range(0, height, rows):
            cross = SCALE * lax.dot_general(
                group,
                src_ref[start : start + rows, :],
                (((1,), (1,)), ((), ())),
                preferred_element_type=jnp.float32,
            )
            cross_ref[:, place : place + rows] = cross
            lse_ref[:, place : place + rows] = log_sum2(cross + bias)
            place += rows


def score_units(group_refs, src_refs, cross_ref, row_ref, done=None):
    top = 0
    for at in range((len(group_refs) + 1) // 2):
        pair = group_refs[2 * at : 2 * at + 2]
        here = slice(top, top + sum(ref.shape[0] for ref in pair))
        score_rows(pair, src_refs, cross_ref.at[here, :], row_ref.at[at : at + 1, :])
        if done is not None:
            done(at, here)
        top = here.stop


def row_pass(groups, sources, with_logw=False):
    count, parts = len(groups), len(sources)
    rows = sum(group.shape[0] for group in groups)
    width = sum(part.shape[0] // EDGE * EDGE for part in sources)
    passes = (count + 1) // 2

    def body(*refs):
        group_refs, src_refs, refs = (
            refs[:count],
            refs[count : count + parts],
            refs[count + parts :],
        )
        kept_ref, lse_ref, *logw_refs, cross_ref, row_ref, sems = refs
        for logw_ref in logw_refs:
            extra = src_refs[0][EDGE:, :].astype(jnp.float32)
            sums = extra[:, :EDGE] + extra[:, EDGE : 2 * EDGE] + extra[:, 2 * EDGE :]
            for quarter in range(HALF // EDGE):
                here = slice(quarter * EDGE, (quarter + 1) * EDGE)
                logw_ref[:, here] = sums[quarter : quarter + 1, :]
        copies = []

        def keep(at, here):
            copies.append(
                pltpu.make_async_copy(cross_ref.at[here, :], kept_ref.at[here, :], sems.at[at])
            )
            copies[-1].start()

        score_units(group_refs, src_refs, cross_ref, row_ref, keep)
        lse_ref[...] = log_sum2(row_ref[...])
        for copy in copies:
            copy.wait()

    small = [jax.ShapeDtypeStruct((1, width), jnp.float32)]
    if with_logw:
        small.append(jax.ShapeDtypeStruct((1, HALF), jnp.float32))
    return pl.pallas_call(
        body,
        in_specs=[IN_VMEM] * (count + parts),
        out_specs=[IN_HBM] + [IN_VMEM] * len(small),
        out_shape=[pltpu.HBM((rows, width), jnp.float32), *small],
        scratch_shapes=[
            pltpu.VMEM((rows, width), jnp.float32),
            pltpu.VMEM((passes, width), jnp.float32),
            pltpu.SemaphoreType.DMA((passes,)),
        ],
        compiler_params=pltpu.CompilerParams(vmem_limit_bytes=VMEM),
        cost_estimate=pl.CostEstimate(flops=1, bytes_accessed=1, transcendentals=0),
        name="rows",
    )(*groups, *sources)


def quarter_places(place_ref):
    return [pl.multiple_of(place_ref[QUARTERS + k] * EDGE, EDGE) for k in range(HALF // EDGE)]


def last_kernel(count, place_ref, *refs):
    group_refs, own_refs, first_refs, round_refs = (
        refs[:count],
        refs[count : count + 1],
        refs[count + 1 : count + 3],
        refs[count + 3 : count + 5],
    )
    first_earlier, *earlier = refs[count + 5 : count + 5 + STEPS]
    near_ref, round_ref, lse_ref, own_row, first_row, round_row = refs[count + 5 + STEPS :]
    score_rows(group_refs[-1:], own_refs, near_ref.at[:, :HALF], own_row)
    score_rows(group_refs[-1:], first_refs, near_ref.at[:, HALF:], first_row)
    score_units(group_refs, round_refs, round_ref, round_row)
    own = log_sum2(jnp.concatenate([own_row[...], *[ref[...] for ref in earlier]], axis=0))
    faced = [
        log_sum2(jnp.concatenate([first_row[...], first_earlier[...]], axis=0)),
        log_sum2(round_row[...]),
    ]
    mine = pl.multiple_of(place_ref[X_HI] * HALF, HALF)
    other = pl.multiple_of((1 - place_ref[X_HI]) * HALF, HALF)
    places = quarter_places(place_ref)
    for peer in range(PEERS):
        lse_ref[peer, :, pl.ds(mine, HALF)] = own
        for at, start in enumerate(places):
            part = faced[at // 2][:, at % 2 * EDGE : (at % 2 + 1) * EDGE]
            lse_ref[peer, :, pl.ds(other + start, EDGE)] = part


def last_pass(place, groups, sources, faced, first_earlier, earlier):
    count = len(groups)
    work = UNIT * (HALF + PART) + ROWS * PART

    def body(*refs):
        last_kernel(count, *refs)

    return pl.pallas_call(
        body,
        in_specs=[IN_SMEM] + [IN_VMEM] * (count + 6 + len(earlier)),
        out_specs=[IN_VMEM] * 3,
        out_shape=[
            pltpu.VMEM((UNIT, HALF + PART), jnp.float32),
            pltpu.VMEM((ROWS, PART), jnp.float32),
            pltpu.VMEM((PEERS, 1, 2 * HALF), jnp.float32),
        ],
        scratch_shapes=[
            pltpu.VMEM((1, HALF), jnp.float32),
            pltpu.VMEM((1, PART), jnp.float32),
            pltpu.VMEM(((count + 1) // 2, PART), jnp.float32),
        ],
        compiler_params=pltpu.CompilerParams(vmem_limit_bytes=VMEM),
        cost_estimate=pl.CostEstimate(
            flops=2 * work * D, bytes_accessed=HALF * D * 4 + work * 4, transcendentals=work
        ),
        name="last_rows",
    )(place, *groups, sources, *faced, first_earlier, *earlier)


def column_kernel(heights, place_ref, *refs):
    own_kept, refs = refs[: len(heights)], refs[len(heights) :]
    first_kept, near_ref, round_ref, partial_ref, sq_ref, logw_ref, faced_logw_ref = refs[:7]
    out_ref, pot_ref, own_held, first_held, peak_ref, total_ref, sems = refs[7:]
    copies, top = [], 0
    for height, own_ref in zip(heights, own_kept):
        for start in range(0, height, UNIT):
            here = slice(top, top + UNIT)
            at = len(copies)
            copies.append(
                (
                    pltpu.make_async_copy(
                        own_ref.at[start : start + UNIT, :], own_held.at[here, :], sems.at[0, at]
                    ),
                    pltpu.make_async_copy(
                        first_kept.at[here, :], first_held.at[here, :], sems.at[1, at]
                    ),
                )
            )
            top += UNIT
    for pair in copies:
        for copy in pair:
            copy.start()
    z, core = place_ref[Z], place_ref[CORE]
    mine = pl.multiple_of(place_ref[X_HI] * HALF, HALF)
    other = pl.multiple_of((1 - place_ref[X_HI]) * HALF, HALF)
    row = log_sum2(partial_ref[:, 0, pl.ds(mine, HALF)])
    own_bias = logw_ref[...] * LOG2E - row
    pot_ref[...] = sq_ref[...] - BACK * row
    own_bias = jnp.broadcast_to(own_bias, (8, HALF))
    faced_bias = [
        faced_logw_ref[:, pl.ds(start, EDGE)] * LOG2E
        - log_sum2(partial_ref[:, 0, pl.ds(other + start, EDGE)])
        for start in quarter_places(place_ref)
    ]
    first_bias = jnp.broadcast_to(jnp.concatenate(faced_bias[:2], axis=1), (8, PART))
    round_bias = jnp.broadcast_to(jnp.concatenate(faced_bias[2:], axis=1), (8, PART))

    def lanes(values):
        return [values[:, k : k + LANES] for k in range(0, values.shape[1], LANES)]

    def sums(pieces, before=None):
        peak = pieces[0] if before is None else jnp.maximum(before[0], pieces[0])
        for piece in pieces[1:]:
            peak = jnp.maximum(peak, piece)
        total = jnp.exp2(pieces[0] - peak)
        for piece in pieces[1:]:
            total = total + jnp.exp2(piece - peak)
        if before is not None:
            total = total + before[1] * jnp.exp2(before[0] - peak)
        return peak, total

    last = REST
    for at in range(0, ROWS, 8):
        rows = slice(at, at + 8)
        pieces = lanes(round_ref[rows, :] + round_bias)
        if at >= last:
            near = near_ref[at - last : at - last + 8, :]
            pieces += lanes(near[:, :HALF] + own_bias) + lanes(near[:, HALF:] + first_bias)
        peak_ref[rows, :], total_ref[rows, :] = sums(pieces)
    for units in (range(2), range(2, 4), range(4, UNITS - 1)):
        for unit in units:
            for copy in copies[unit]:
                copy.wait()
        for at in range(units.start * UNIT, units.stop * UNIT, 8):
            rows = slice(at, at + 8)
            pieces = lanes(own_held[rows, :] + own_bias)
            pieces += lanes(first_held[rows, :] + first_bias)
            before = peak_ref[rows, :], total_ref[rows, :]
            peak_ref[rows, :], total_ref[rows, :] = sums(pieces, before)
    side = 2 * core - 1
    for unit in range(UNITS):
        rows = slice(unit * UNIT, (unit + 1) * UNIT)
        peak, total = peak_ref[rows, :].T, total_ref[rows, :].T
        highest = jnp.max(peak, axis=0, keepdims=True)
        total = jnp.sum(total * jnp.exp2(peak - highest), axis=0, keepdims=True)
        lse = highest + jnp.log2(total)
        if unit == 0:
            first, second = 2 * z + core, 2 * z + 1 - core
        else:
            step = (unit + 1) // 2
            chip = lax.rem(z + UNITS + (side if unit % 2 else -side) * step, UNITS)
            first, second = 2 * chip, 2 * chip + 1
        out_ref[pl.ds(first, 1)] = lse[:, :OWN].reshape(1, 1, OWN)
        out_ref[pl.ds(second, 1)] = lse[:, OWN:].reshape(1, 1, OWN)


def column_pass(place, own_crosses, first_cross, near, round_cross, partial, *rows):
    heights = [cross.shape[0] for cross in own_crosses]

    def body(*refs):
        column_kernel(heights, *refs)

    return pl.pallas_call(
        body,
        in_specs=[IN_SMEM] + [IN_HBM] * (len(own_crosses) + 1) + [IN_VMEM] * 6,
        out_specs=[IN_VMEM] * 2,
        out_shape=[
            jax.ShapeDtypeStruct((PEERS, 1, OWN), jnp.float32),
            jax.ShapeDtypeStruct((1, HALF), jnp.float32),
        ],
        scratch_shapes=[
            pltpu.VMEM((REST, HALF), jnp.float32),
            pltpu.VMEM((REST, PART), jnp.float32),
            pltpu.VMEM((ROWS, LANES), jnp.float32),
            pltpu.VMEM((ROWS, LANES), jnp.float32),
            pltpu.SemaphoreType.DMA((2, UNITS - 1)),
        ],
        compiler_params=pltpu.CompilerParams(vmem_limit_bytes=VMEM),
        cost_estimate=pl.CostEstimate(
            flops=12 * ROWS * HALF, bytes_accessed=ROWS * HALF * 8, transcendentals=2 * ROWS * HALF
        ),
        name="columns",
    )(
        place,
        *in_hbm(*own_crosses, first_cross),
        pltpu.with_memory_space_constraint(near, pltpu.VMEM),
        pltpu.with_memory_space_constraint(round_cross, pltpu.VMEM),
        partial,
        *[row.reshape(1, HALF) for row in rows],
    )


def on_device(sources, targets, potential_in, source_logw, target_logw):
    x_lo, x_hi, odd = lax.axis_index("x_lo"), lax.axis_index("x_hi"), lax.axis_index("y") % 2
    quarters = [
        2 * odd + x_lo,
        2 * (1 - odd) + 1 - x_lo,
        2 * (1 - odd) + x_lo,
        2 * odd + 1 - x_lo,
    ]
    sent, sent_next = 2 * odd + 1 - x_lo, 2 * (1 - odd) + x_lo
    place = jnp.stack(
        [x_hi, lax.axis_index("z"), lax.axis_index("core"), *quarters, sent]
    ).astype(jnp.int32)
    own, tgt_sq, edge = pack(
        place, sources, targets, potential_in, target_logw, source_logw
    )
    straight = facing(edge)
    same, cross_core = onward(own), onward_across(own)
    opposite = facing(lax.dynamic_slice(sources, (sent_next * EDGE, 0), (EDGE, D)))
    beside = other_core(own)

    first = lax.axis_index("core") == 0
    unit = jnp.concatenate(
        [jnp.where(first, same, cross_core), jnp.where(first, cross_core, same)], axis=0
    )
    src_sq = jnp.sum(jnp.square(sources.astype(jnp.float32)), axis=1)
    groups, crosses, lses = [], [], []
    pending = [own, beside]
    for step in (1, 2, 3):
        following = onward(unit)
        beside = other_core(unit)
        if step == 1:
            by_y, by_x = beside_y(straight), beside_x(straight)
        cross, lse = row_pass(pending, [sources])
        groups += pending
        crosses.append(cross)
        if step == 1:
            following, lse, src_sq = lax.optimization_barrier((following, lse, src_sq))
        elif step == 2:
            following, lse, opposite = lax.optimization_barrier((following, lse, opposite))
        else:
            following, lse = lax.optimization_barrier((following, lse))
        lses.append(lse)
        pending = [unit, beside]
        unit = following
    cross, lse = row_pass(pending, [sources])
    groups += pending
    crosses.append(cross)
    first_cross, first_lse, faced_logw = row_pass(groups, [straight, opposite], True)
    unit, lse, first_lse = lax.optimization_barrier((unit, lse, first_lse))
    lses.append(lse)
    groups.append(unit)
    near, round_cross, shared = last_pass(
        place, groups, sources, [straight, opposite, by_y, by_x], first_lse, lses
    )

    partial = lax.all_to_all(shared, ("y", "x_lo", "x_hi"), 0, 0, tiled=True)
    columns, source_potential = column_pass(
        place, crosses, first_cross, near, round_cross, partial, src_sq, source_logw, faced_logw
    )
    gathered = lax.all_to_all(columns, ("z", "core"), 0, 0, tiled=True)
    final = log_sum2(gathered.reshape(PEERS, OWN)).reshape(OWN)
    potential_out = tgt_sq.reshape(OWN) - BACK * final
    return (source_potential.reshape(HALF), potential_out)


def solution(mesh):
    every = ("y", "x_lo", "z", "x_hi", "core")
    blk = ("z", "x_hi", "core")
    fine = Mesh(mesh.devices.reshape(4, 2, 8, 2, 2), every)
    in_specs = (P(blk, None), P(every, None), P(every), P(blk), P(every))
    out_specs = (P(blk), P(every))
    return jax.shard_map(
        on_device, mesh=fine, in_specs=in_specs, out_specs=out_specs, check_vma=False
    )
```

```python
import math

import jax
import jax.numpy as jnp
from jax import lax
from jax.experimental import pallas as pl
from jax.experimental.pallas import tpu as pltpu
from jax.sharding import Mesh, PartitionSpec as P

EPSILON = 0.05
LOG2E = math.log2(math.e)
SCALE = 2.0 / EPSILON * LOG2E
BACK = EPSILON * math.log(2.0)

D = 768
PAD = 128
OWN = 64
UNIT = 2 * OWN
UNITS = 8
ROWS = UNIT * UNITS
HALF = 1024
BLOCK = 512
LANES = 128
PEERS = 16
X_HI, Z, CORE, QUARTERS, SENT = 0, 1, 2, 3, 7
PART = HALF // 2
PASSES = 4
VMEM = 12 * 1024 * 1024
EDGE = HALF // 4
EXTRA = 16
REST = ROWS - UNIT
IN_VMEM = pl.BlockSpec(memory_space=pltpu.VMEM)
IN_HBM = pl.BlockSpec(memory_space=pl.ANY)
IN_SMEM = pl.BlockSpec(memory_space=pltpu.SMEM)


def whole(*shape):
    return pl.BlockSpec(shape, lambda i: (0,) * len(shape))


def onward(value):
    count = lax.axis_size("z")
    up = [(2 * i, 2 * ((i + 1) % count)) for i in range(count)]
    down = [(2 * i + 1, 2 * ((i - 1) % count) + 1) for i in range(count)]
    return lax.ppermute(value, ("z", "core"), up + down)


def onward_across(value):
    count = lax.axis_size("z")
    up = [(2 * i + 1, 2 * ((i + 1) % count)) for i in range(count)]
    down = [(2 * i, 2 * ((i - 1) % count) + 1) for i in range(count)]
    return lax.ppermute(value, ("z", "core"), up + down)


def other_core(value):
    return lax.ppermute(value, "core", [(0, 1), (1, 0)])


def facing(value):
    return lax.ppermute(value, ("x_lo", "x_hi"), [(0, 3), (3, 0), (1, 2), (2, 1)])


def beside_x(value):
    return lax.ppermute(value, "x_lo", [(0, 1), (1, 0)])


def beside_y(value):
    return lax.ppermute(value, "y", [(0, 1), (1, 0), (2, 3), (3, 2)])


def log_sum2(values):
    peak = jnp.max(values, axis=0, keepdims=True)
    return peak + jnp.log2(jnp.sum(jnp.exp2(values - peak), axis=0, keepdims=True))


def split(values):
    high = values.astype(jnp.bfloat16).astype(jnp.float32)
    rest = values - high
    middle = rest.astype(jnp.bfloat16).astype(jnp.float32)
    return high, middle, rest - middle


def pack_kernel(place_ref, src_hbm, tgt_hbm, pot_hbm, logw_hbm, *refs):
    src_logw_hbm, own_ref, sq_ref, edge_ref, tgt_ref, pot_ref, logw_ref, src_logw_ref, sems = refs
    copies = [
        pltpu.make_async_copy(source, target, sems.at[at])
        for at, (source, target) in enumerate(
            (
                (tgt_hbm, tgt_ref),
                (pot_hbm, pot_ref),
                (logw_hbm, logw_ref),
                (src_logw_hbm, src_logw_ref),
            )
        )
    ]
    for copy in copies:
        copy.start()
    start = pl.multiple_of(place_ref[SENT] * EDGE, EDGE)
    edge = pltpu.make_async_copy(
        src_hbm.at[pl.ds(start, EDGE), :], edge_ref.at[:EDGE, :], sems.at[4]
    )
    edge.start()
    for copy in copies:
        copy.wait()
    tgt = tgt_ref[...]
    wide = tgt.astype(jnp.float32)
    sq = jnp.sum(wide * wide, axis=1, keepdims=True)
    diagonal = lax.broadcasted_iota(jnp.int32, (OWN, OWN), 0) == lax.broadcasted_iota(
        jnp.int32, (OWN, OWN), 1
    )

    def upright(row):
        return jnp.sum(jnp.where(diagonal, row, 0.0), axis=1, keepdims=True)

    sq_ref[...] = jnp.sum(jnp.where(diagonal, sq, 0.0), axis=0, keepdims=True)
    bias = (upright(logw_ref[...]) + (upright(pot_ref[...]) - sq) / EPSILON) * LOG2E
    high, middle, low = split(bias)
    lane = lax.broadcasted_iota(jnp.int32, (OWN, PAD), 1)
    pieces = jnp.where(lane == 0, high, 0.0)
    pieces = jnp.where(lane == 1, middle, pieces)
    pieces = jnp.where(lane == 2, low, pieces)
    own_ref[:, :D] = tgt
    own_ref[:, D:] = pieces.astype(jnp.bfloat16)
    line = lax.broadcasted_iota(jnp.int32, (EXTRA, D), 0)
    extra = jnp.zeros((EXTRA, D), jnp.float32)
    for quarter in range(HALF // EDGE):
        part = src_logw_ref[:, quarter * EDGE : (quarter + 1) * EDGE]
        row = jnp.concatenate(split(part), axis=1)
        extra = jnp.where(line == quarter, row, extra)
    edge_ref[EDGE:, :] = extra.astype(jnp.bfloat16)
    edge.wait()


def in_hbm(*values):
    return [pltpu.with_memory_space_constraint(value, pltpu.HBM) for value in values]


def pack(place, sources, targets, potential, logw, src_logw):
    return pl.pallas_call(
        pack_kernel,
        in_specs=[IN_SMEM] + [IN_HBM] * 5,
        out_specs=[IN_VMEM] * 3,
        out_shape=[
            jax.ShapeDtypeStruct((OWN, D + PAD), jnp.bfloat16),
            jax.ShapeDtypeStruct((1, OWN), jnp.float32),
            jax.ShapeDtypeStruct((EDGE + EXTRA, D), jnp.bfloat16),
        ],
        scratch_shapes=[
            pltpu.VMEM((OWN, D), jnp.bfloat16),
            pltpu.VMEM((1, OWN), jnp.float32),
            pltpu.VMEM((1, OWN), jnp.float32),
            pltpu.VMEM((1, HALF), jnp.float32),
            pltpu.SemaphoreType.DMA((5,)),
        ],
        compiler_params=pltpu.CompilerParams(vmem_limit_bytes=VMEM),
        name="pack",
    )(
        place,
        *in_hbm(
            sources,
            targets,
            potential.reshape(1, OWN),
            logw.reshape(1, OWN),
            src_logw.reshape(1, HALF),
        ),
    )


def score_rows(group_refs, src_refs, cross_ref, lse_ref):
    group = jnp.concatenate([ref[...] for ref in group_refs], axis=0)
    pieces = group[:, D:].astype(jnp.float32)
    bias = pieces[:, 0:1] + pieces[:, 1:2] + pieces[:, 2:3]
    group = group[:, :D]
    place, totals = 0, []
    for src_ref in src_refs:
        height = src_ref.shape[0] // EDGE * EDGE
        rows = min(BLOCK, height)
        for start in range(0, height, rows):
            cross = SCALE * lax.dot_general(
                group,
                src_ref[start : start + rows, :],
                (((1,), (1,)), ((), ())),
                preferred_element_type=jnp.float32,
            )
            cross_ref[:, place : place + rows] = cross
            totals.append(log_sum2(cross + bias))
            place += rows
    lse_ref[...] = jnp.concatenate(totals, axis=1)


def score_units(group_refs, src_refs, cross_ref, row_ref, done=None):
    top = 0
    for at in range((len(group_refs) + 1) // 2):
        pair = group_refs[2 * at : 2 * at + 2]
        here = slice(top, top + sum(ref.shape[0] for ref in pair))
        score_rows(pair, src_refs, cross_ref.at[here, :], row_ref.at[at : at + 1, :])
        if done is not None:
            done(at, here)
        top = here.stop


def row_pass(groups, sources, faced=(), late=0):
    count, parts = len(groups), len(faced)
    tops = [sum(group.shape[0] for group in groups[:at]) for at in range(count + 1)]
    own_from = count - late if parts else 0
    own_rows, all_rows = tops[-1] - tops[own_from], tops[-1]
    own_passes, passes = (count - own_from + 1) // 2, (count + 1) // 2
    width = sum(part.shape[0] // EDGE * EDGE for part in faced)

    def body(*refs):
        group_refs, src_ref = refs[:count], refs[count]
        faced_refs, refs = refs[count + 1 : count + 1 + parts], refs[count + 1 + parts :]
        if parts:
            kept_ref, lse_ref, faced_kept, faced_lse, logw_ref, *refs = refs
            cross_ref, row_ref, sems, faced_cross, faced_row, faced_sems = refs
            extra = faced_refs[0][EDGE:, :].astype(jnp.float32)
            sums = extra[:, :EDGE] + extra[:, EDGE : 2 * EDGE] + extra[:, 2 * EDGE :]
            for quarter in range(HALF // EDGE):
                here = slice(quarter * EDGE, (quarter + 1) * EDGE)
                logw_ref[:, here] = sums[quarter : quarter + 1, :]
        else:
            kept_ref, lse_ref, cross_ref, row_ref, sems = refs
        copies = []

        def keeper(held_ref, kept_ref, sems):
            def keep(at, here):
                copy = pltpu.make_async_copy(held_ref.at[here, :], kept_ref.at[here, :], sems.at[at])
                copy.start()
                copies.append(copy)

            return keep

        score_units(
            group_refs[own_from:], [src_ref], cross_ref, row_ref, keeper(cross_ref, kept_ref, sems)
        )
        if parts:
            keep = keeper(faced_cross, faced_kept, faced_sems)
            score_units(group_refs, faced_refs, faced_cross, faced_row, keep)
            faced_lse[...] = log_sum2(faced_row[...])
        lse_ref[...] = log_sum2(row_ref[...])
        for copy in copies:
            copy.wait()

    out_shape = [
        pltpu.HBM((own_rows, HALF), jnp.float32),
        jax.ShapeDtypeStruct((1, HALF), jnp.float32),
    ]
    scratch = [
        pltpu.VMEM((own_rows, HALF), jnp.float32),
        pltpu.VMEM((own_passes, HALF), jnp.float32),
        pltpu.SemaphoreType.DMA((own_passes,)),
    ]
    if parts:
        out_shape += [
            pltpu.HBM((all_rows, width), jnp.float32),
            jax.ShapeDtypeStruct((1, width), jnp.float32),
            jax.ShapeDtypeStruct((1, HALF), jnp.float32),
        ]
        scratch += [
            pltpu.VMEM((all_rows, width), jnp.float32),
            pltpu.VMEM((passes, width), jnp.float32),
            pltpu.SemaphoreType.DMA((passes,)),
        ]
    return pl.pallas_call(
        body,
        in_specs=[IN_VMEM] * (count + 1 + parts),
        out_specs=[IN_HBM, IN_VMEM] + [IN_HBM, IN_VMEM, IN_VMEM] * (parts > 0),
        out_shape=out_shape,
        scratch_shapes=scratch,
        compiler_params=pltpu.CompilerParams(vmem_limit_bytes=VMEM),
        cost_estimate=pl.CostEstimate(flops=1, bytes_accessed=1, transcendentals=0),
        name="rows",
    )(*groups, sources, *faced)


def quarter_places(place_ref):
    return [pl.multiple_of(place_ref[QUARTERS + k] * EDGE, EDGE) for k in range(HALF // EDGE)]


def last_kernel(count, place_ref, *refs):
    group_refs, own_refs, first_refs, round_refs = (
        refs[:count],
        refs[count : count + 1],
        refs[count + 1 : count + 3],
        refs[count + 3 : count + 5],
    )
    first_earlier, *earlier = refs[count + 5 : count + 5 + PASSES]
    near_ref, round_ref, lse_ref, own_row, first_row, round_row = refs[count + 5 + PASSES :]
    score_rows(group_refs[-1:], own_refs, near_ref.at[:, :HALF], own_row)
    score_rows(group_refs[-1:], first_refs, near_ref.at[:, HALF:], first_row)
    score_units(group_refs, round_refs, round_ref, round_row)
    own = log_sum2(jnp.concatenate([own_row[...], *[ref[...] for ref in earlier]], axis=0))
    faced = [
        log_sum2(jnp.concatenate([first_row[...], first_earlier[...]], axis=0)),
        log_sum2(round_row[...]),
    ]
    mine = pl.multiple_of(place_ref[X_HI] * HALF, HALF)
    other = pl.multiple_of((1 - place_ref[X_HI]) * HALF, HALF)
    places = quarter_places(place_ref)
    for peer in range(PEERS):
        lse_ref[peer, :, pl.ds(mine, HALF)] = own
        for at, start in enumerate(places):
            part = faced[at // 2][:, at % 2 * EDGE : (at % 2 + 1) * EDGE]
            lse_ref[peer, :, pl.ds(other + start, EDGE)] = part


def last_pass(place, groups, sources, faced, first_earlier, earlier):
    count = len(groups)
    work = UNIT * (HALF + PART) + ROWS * PART

    def body(*refs):
        last_kernel(count, *refs)

    return pl.pallas_call(
        body,
        in_specs=[IN_SMEM] + [IN_VMEM] * (count + 6 + len(earlier)),
        out_specs=[IN_VMEM] * 3,
        out_shape=[
            pltpu.VMEM((UNIT, HALF + PART), jnp.float32),
            pltpu.VMEM((ROWS, PART), jnp.float32),
            pltpu.VMEM((PEERS, 1, 2 * HALF), jnp.float32),
        ],
        scratch_shapes=[
            pltpu.VMEM((1, HALF), jnp.float32),
            pltpu.VMEM((1, PART), jnp.float32),
            pltpu.VMEM(((count + 1) // 2, PART), jnp.float32),
        ],
        compiler_params=pltpu.CompilerParams(vmem_limit_bytes=VMEM),
        cost_estimate=pl.CostEstimate(
            flops=2 * work * D, bytes_accessed=HALF * D * 4 + work * 4, transcendentals=work
        ),
        name="last_rows",
    )(place, *groups, sources, *faced, first_earlier, *earlier)


def column_kernel(heights, place_ref, *refs):
    own_kept, refs = refs[: len(heights)], refs[len(heights) :]
    first_kept, near_ref, round_ref, partial_ref, sq_ref, logw_ref, faced_logw_ref = refs[:7]
    out_ref, pot_ref, own_held, first_held, peak_ref, total_ref, sems = refs[7:]
    copies, top = [], 0
    for height, own_ref in zip(heights, own_kept):
        for start in range(0, height, UNIT):
            here = slice(top, top + UNIT)
            at = len(copies)
            copies.append(
                (
                    pltpu.make_async_copy(
                        own_ref.at[start : start + UNIT, :], own_held.at[here, :], sems.at[0, at]
                    ),
                    pltpu.make_async_copy(
                        first_kept.at[here, :], first_held.at[here, :], sems.at[1, at]
                    ),
                )
            )
            top += UNIT
    for pair in copies:
        for copy in pair:
            copy.start()
    z, core = place_ref[Z], place_ref[CORE]
    mine = pl.multiple_of(place_ref[X_HI] * HALF, HALF)
    other = pl.multiple_of((1 - place_ref[X_HI]) * HALF, HALF)
    row = log_sum2(partial_ref[:, 0, pl.ds(mine, HALF)])
    own_bias = logw_ref[...] * LOG2E - row
    pot_ref[...] = sq_ref[...] - BACK * row
    own_bias = jnp.broadcast_to(own_bias, (8, HALF))
    faced_bias = [
        faced_logw_ref[:, pl.ds(start, EDGE)] * LOG2E
        - log_sum2(partial_ref[:, 0, pl.ds(other + start, EDGE)])
        for start in quarter_places(place_ref)
    ]
    first_bias = jnp.broadcast_to(jnp.concatenate(faced_bias[:2], axis=1), (8, PART))
    round_bias = jnp.broadcast_to(jnp.concatenate(faced_bias[2:], axis=1), (8, PART))

    def lanes(values):
        return [values[:, k : k + LANES] for k in range(0, values.shape[1], LANES)]

    def sums(pieces, before=None):
        peak = pieces[0] if before is None else jnp.maximum(before[0], pieces[0])
        for piece in pieces[1:]:
            peak = jnp.maximum(peak, piece)
        total = jnp.exp2(pieces[0] - peak)
        for piece in pieces[1:]:
            total = total + jnp.exp2(piece - peak)
        if before is not None:
            total = total + before[1] * jnp.exp2(before[0] - peak)
        return peak, total

    last = REST
    for at in range(0, ROWS, 8):
        rows = slice(at, at + 8)
        pieces = lanes(round_ref[rows, :] + round_bias)
        if at >= last:
            near = near_ref[at - last : at - last + 8, :]
            pieces += lanes(near[:, :HALF] + own_bias) + lanes(near[:, HALF:] + first_bias)
        peak_ref[rows, :], total_ref[rows, :] = sums(pieces)
    for units in (range(2), range(2, 4), range(4, UNITS - 1)):
        for unit in units:
            for copy in copies[unit]:
                copy.wait()
        for at in range(units.start * UNIT, units.stop * UNIT, 8):
            rows = slice(at, at + 8)
            pieces = lanes(own_held[rows, :] + own_bias)
            pieces += lanes(first_held[rows, :] + first_bias)
            before = peak_ref[rows, :], total_ref[rows, :]
            peak_ref[rows, :], total_ref[rows, :] = sums(pieces, before)
    side = 2 * core - 1
    for unit in range(UNITS):
        rows = slice(unit * UNIT, (unit + 1) * UNIT)
        peak, total = peak_ref[rows, :].T, total_ref[rows, :].T
        highest = jnp.max(peak, axis=0, keepdims=True)
        total = jnp.sum(total * jnp.exp2(peak - highest), axis=0, keepdims=True)
        lse = highest + jnp.log2(total)
        if unit == 0:
            first, second = 2 * z + core, 2 * z + 1 - core
        else:
            step = (unit + 1) // 2
            chip = lax.rem(z + UNITS + (side if unit % 2 else -side) * step, UNITS)
            first, second = 2 * chip, 2 * chip + 1
        out_ref[pl.ds(first, 1)] = lse[:, :OWN].reshape(1, 1, OWN)
        out_ref[pl.ds(second, 1)] = lse[:, OWN:].reshape(1, 1, OWN)


def column_pass(place, own_crosses, first_cross, near, round_cross, partial, *rows):
    heights = [cross.shape[0] for cross in own_crosses]

    def body(*refs):
        column_kernel(heights, *refs)

    return pl.pallas_call(
        body,
        in_specs=[IN_SMEM] + [IN_HBM] * (len(own_crosses) + 1) + [IN_VMEM] * 6,
        out_specs=[IN_VMEM] * 2,
        out_shape=[
            jax.ShapeDtypeStruct((PEERS, 1, OWN), jnp.float32),
            jax.ShapeDtypeStruct((1, HALF), jnp.float32),
        ],
        scratch_shapes=[
            pltpu.VMEM((REST, HALF), jnp.float32),
            pltpu.VMEM((REST, PART), jnp.float32),
            pltpu.VMEM((ROWS, LANES), jnp.float32),
            pltpu.VMEM((ROWS, LANES), jnp.float32),
            pltpu.SemaphoreType.DMA((2, UNITS - 1)),
        ],
        compiler_params=pltpu.CompilerParams(vmem_limit_bytes=VMEM),
        cost_estimate=pl.CostEstimate(
            flops=12 * ROWS * HALF, bytes_accessed=ROWS * HALF * 8, transcendentals=2 * ROWS * HALF
        ),
        name="columns",
    )(
        place,
        *in_hbm(*own_crosses, first_cross),
        pltpu.with_memory_space_constraint(near, pltpu.VMEM),
        pltpu.with_memory_space_constraint(round_cross, pltpu.VMEM),
        partial,
        *[row.reshape(1, HALF) for row in rows],
    )


def on_device(sources, targets, potential_in, source_logw, target_logw):
    x_lo, x_hi, odd = lax.axis_index("x_lo"), lax.axis_index("x_hi"), lax.axis_index("y") % 2
    quarters = [
        2 * odd + x_lo,
        2 * (1 - odd) + 1 - x_lo,
        2 * (1 - odd) + x_lo,
        2 * odd + 1 - x_lo,
    ]
    sent, sent_next = 2 * odd + 1 - x_lo, 2 * (1 - odd) + x_lo
    place = jnp.stack(
        [x_hi, lax.axis_index("z"), lax.axis_index("core"), *quarters, sent]
    ).astype(jnp.int32)
    own, tgt_sq, edge = pack(
        place, sources, targets, potential_in, target_logw, source_logw
    )
    straight = facing(edge)
    same, cross_core = onward(own), onward_across(own)
    opposite = facing(lax.dynamic_slice(sources, (sent_next * EDGE, 0), (EDGE, D)))
    beside = other_core(own)

    first = lax.axis_index("core") == 0
    unit = jnp.concatenate(
        [jnp.where(first, same, cross_core), jnp.where(first, cross_core, same)], axis=0
    )
    src_sq = jnp.sum(jnp.square(sources.astype(jnp.float32)), axis=1)
    groups, crosses, lses = [own, beside], [], []
    for step in (1, 2):
        following = onward(unit)
        beside = other_core(unit)
        if step == 1:
            by_y, by_x = beside_y(straight), beside_x(straight)
        cross, lse = row_pass(groups[-2:], sources)
        crosses.append(cross)
        lses.append(lse)
        groups += [unit, beside]
        if step == 1:
            unit, lses[0], src_sq = lax.optimization_barrier((following, lse, src_sq))
        else:
            unit, lses[1] = lax.optimization_barrier((following, lse))
            groups[-1], opposite = lax.optimization_barrier((groups[-1], opposite))
    groups += [unit, other_core(unit)]
    following = onward(unit)
    cross, lse, first_cross, first_lse, faced_logw = row_pass(
        groups, sources, [straight, opposite], 4
    )
    crosses.append(cross)
    unit, lse, first_lse = lax.optimization_barrier((following, lse, first_lse))
    lses.append(lse)
    groups.append(unit)
    near, round_cross, shared = last_pass(
        place, groups, sources, [straight, opposite, by_y, by_x], first_lse, lses
    )

    partial = lax.all_to_all(shared, ("y", "x_lo", "x_hi"), 0, 0, tiled=True)
    columns, source_potential = column_pass(
        place, crosses, first_cross, near, round_cross, partial, src_sq, source_logw, faced_logw
    )
    gathered = lax.all_to_all(columns, ("z", "core"), 0, 0, tiled=True)
    final = log_sum2(gathered.reshape(PEERS, OWN)).reshape(OWN)
    potential_out = tgt_sq.reshape(OWN) - BACK * final
    return (source_potential.reshape(HALF), potential_out)


def solution(mesh):
    every = ("y", "x_lo", "z", "x_hi", "core")
    blk = ("z", "x_hi", "core")
    fine = Mesh(mesh.devices.reshape(4, 2, 8, 2, 2), every)
    in_specs = (P(blk, None), P(every, None), P(every), P(blk), P(every))
    out_specs = (P(blk), P(every))
    return jax.shard_map(
        on_device, mesh=fine, in_specs=in_specs, out_specs=out_specs, check_vma=False
    )
```

```python
import math

import jax
import jax.numpy as jnp
from jax import lax
from jax.experimental import pallas as pl
from jax.experimental.pallas import tpu as pltpu
from jax.sharding import Mesh, PartitionSpec as P

EPSILON = 0.05
LOG2E = math.log2(math.e)
SCALE = 2.0 / EPSILON * LOG2E
BACK = EPSILON * math.log(2.0)

D = 768
PAD = 128
OWN = 64
UNIT = 2 * OWN
UNITS = 8
ROWS = UNIT * UNITS
HALF = 1024
BLOCK = 512
LANES = 128
PEERS = 16
X_HI, Z, CORE, QUARTERS, SENT = 0, 1, 2, 3, 7
PART = HALF // 2
PASSES = 4
VMEM = 12 * 1024 * 1024
EDGE = HALF // 4
EXTRA = 16
REST = ROWS - UNIT
IN_VMEM = pl.BlockSpec(memory_space=pltpu.VMEM)
IN_HBM = pl.BlockSpec(memory_space=pl.ANY)
IN_SMEM = pl.BlockSpec(memory_space=pltpu.SMEM)


def whole(*shape):
    return pl.BlockSpec(shape, lambda i: (0,) * len(shape))


def onward(value):
    count = lax.axis_size("z")
    up = [(2 * i + 1, 2 * ((i + 1) % count) + 1) for i in range(count)]
    down = [(2 * i, 2 * ((i - 1) % count)) for i in range(count)]
    return lax.ppermute(value, ("z", "core"), up + down)


def onward_across(value):
    count = lax.axis_size("z")
    up = [(2 * i, 2 * ((i + 1) % count) + 1) for i in range(count)]
    down = [(2 * i + 1, 2 * ((i - 1) % count)) for i in range(count)]
    return lax.ppermute(value, ("z", "core"), up + down)


def other_core(value):
    return lax.ppermute(value, "core", [(0, 1), (1, 0)])


def facing(value):
    return lax.ppermute(value, ("x_lo", "x_hi"), [(0, 3), (3, 0), (1, 2), (2, 1)])


def beside_x(value):
    return lax.ppermute(value, "x_lo", [(0, 1), (1, 0)])


def beside_y(value):
    return lax.ppermute(value, "y", [(0, 1), (1, 0), (2, 3), (3, 2)])


def log_sum2(values):
    peak = jnp.max(values, axis=0, keepdims=True)
    return peak + jnp.log2(jnp.sum(jnp.exp2(values - peak), axis=0, keepdims=True))


def split(values):
    high = values.astype(jnp.bfloat16).astype(jnp.float32)
    rest = values - high
    middle = rest.astype(jnp.bfloat16).astype(jnp.float32)
    return high, middle, rest - middle


def pack_kernel(place_ref, src_hbm, tgt_hbm, pot_hbm, logw_hbm, *refs):
    src_logw_hbm, own_ref, sq_ref, edge_ref, tgt_ref, pot_ref, logw_ref, src_logw_ref, sems = refs
    copies = [
        pltpu.make_async_copy(source, target, sems.at[at])
        for at, (source, target) in enumerate(
            (
                (tgt_hbm, tgt_ref),
                (pot_hbm, pot_ref),
                (logw_hbm, logw_ref),
                (src_logw_hbm, src_logw_ref),
            )
        )
    ]
    for copy in copies:
        copy.start()
    start = pl.multiple_of(place_ref[SENT] * EDGE, EDGE)
    edge = pltpu.make_async_copy(
        src_hbm.at[pl.ds(start, EDGE), :], edge_ref.at[:EDGE, :], sems.at[4]
    )
    edge.start()
    for copy in copies:
        copy.wait()
    tgt = tgt_ref[...]
    wide = tgt.astype(jnp.float32)
    sq = jnp.sum(wide * wide, axis=1, keepdims=True)
    diagonal = lax.broadcasted_iota(jnp.int32, (OWN, OWN), 0) == lax.broadcasted_iota(
        jnp.int32, (OWN, OWN), 1
    )

    def upright(row):
        return jnp.sum(jnp.where(diagonal, row, 0.0), axis=1, keepdims=True)

    sq_ref[...] = jnp.sum(jnp.where(diagonal, sq, 0.0), axis=0, keepdims=True)
    bias = (upright(logw_ref[...]) + (upright(pot_ref[...]) - sq) / EPSILON) * LOG2E
    high, middle, low = split(bias)
    lane = lax.broadcasted_iota(jnp.int32, (OWN, PAD), 1)
    pieces = jnp.where(lane == 0, high, 0.0)
    pieces = jnp.where(lane == 1, middle, pieces)
    pieces = jnp.where(lane == 2, low, pieces)
    own_ref[:, :D] = tgt
    own_ref[:, D:] = pieces.astype(jnp.bfloat16)
    line = lax.broadcasted_iota(jnp.int32, (EXTRA, D), 0)
    extra = jnp.zeros((EXTRA, D), jnp.float32)
    for quarter in range(HALF // EDGE):
        part = src_logw_ref[:, quarter * EDGE : (quarter + 1) * EDGE]
        row = jnp.concatenate(split(part), axis=1)
        extra = jnp.where(line == quarter, row, extra)
    edge_ref[EDGE:, :] = extra.astype(jnp.bfloat16)
    edge.wait()


def in_hbm(*values):
    return [pltpu.with_memory_space_constraint(value, pltpu.HBM) for value in values]


def pack(place, sources, targets, potential, logw, src_logw):
    return pl.pallas_call(
        pack_kernel,
        in_specs=[IN_SMEM] + [IN_HBM] * 5,
        out_specs=[IN_VMEM] * 3,
        out_shape=[
            jax.ShapeDtypeStruct((OWN, D + PAD), jnp.bfloat16),
            jax.ShapeDtypeStruct((1, OWN), jnp.float32),
            jax.ShapeDtypeStruct((EDGE + EXTRA, D), jnp.bfloat16),
        ],
        scratch_shapes=[
            pltpu.VMEM((OWN, D), jnp.bfloat16),
            pltpu.VMEM((1, OWN), jnp.float32),
            pltpu.VMEM((1, OWN), jnp.float32),
            pltpu.VMEM((1, HALF), jnp.float32),
            pltpu.SemaphoreType.DMA((5,)),
        ],
        compiler_params=pltpu.CompilerParams(vmem_limit_bytes=VMEM),
        name="pack",
    )(
        place,
        *in_hbm(
            sources,
            targets,
            potential.reshape(1, OWN),
            logw.reshape(1, OWN),
            src_logw.reshape(1, HALF),
        ),
    )


def score_rows(group_refs, src_refs, cross_ref, lse_ref):
    group = jnp.concatenate([ref[...] for ref in group_refs], axis=0)
    pieces = group[:, D:].astype(jnp.float32)
    bias = pieces[:, 0:1] + pieces[:, 1:2] + pieces[:, 2:3]
    group = group[:, :D]
    place, totals = 0, []
    for src_ref in src_refs:
        height = src_ref.shape[0] // EDGE * EDGE
        rows = min(BLOCK, height)
        for start in range(0, height, rows):
            cross = SCALE * lax.dot_general(
                group,
                src_ref[start : start + rows, :],
                (((1,), (1,)), ((), ())),
                preferred_element_type=jnp.float32,
            )
            cross_ref[:, place : place + rows] = cross
            totals.append(log_sum2(cross + bias))
            place += rows
    lse_ref[...] = jnp.concatenate(totals, axis=1)


def score_units(group_refs, src_refs, cross_ref, row_ref, done=None):
    top = 0
    for at in range((len(group_refs) + 1) // 2):
        pair = group_refs[2 * at : 2 * at + 2]
        here = slice(top, top + sum(ref.shape[0] for ref in pair))
        score_rows(pair, src_refs, cross_ref.at[here, :], row_ref.at[at : at + 1, :])
        if done is not None:
            done(at, here)
        top = here.stop


def row_pass(groups, sources, faced=(), late=0):
    count, parts = len(groups), len(faced)
    tops = [sum(group.shape[0] for group in groups[:at]) for at in range(count + 1)]
    own_from = count - late if parts else 0
    own_rows, all_rows = tops[-1] - tops[own_from], tops[-1]
    own_passes, passes = (count - own_from + 1) // 2, (count + 1) // 2
    width = sum(part.shape[0] // EDGE * EDGE for part in faced)

    def body(*refs):
        group_refs, src_ref = refs[:count], refs[count]
        faced_refs, refs = refs[count + 1 : count + 1 + parts], refs[count + 1 + parts :]
        if parts:
            kept_ref, lse_ref, faced_kept, faced_lse, logw_ref, *refs = refs
            cross_ref, row_ref, sems, faced_cross, faced_row, faced_sems = refs
            extra = faced_refs[0][EDGE:, :].astype(jnp.float32)
            sums = extra[:, :EDGE] + extra[:, EDGE : 2 * EDGE] + extra[:, 2 * EDGE :]
            for quarter in range(HALF // EDGE):
                here = slice(quarter * EDGE, (quarter + 1) * EDGE)
                logw_ref[:, here] = sums[quarter : quarter + 1, :]
        else:
            kept_ref, lse_ref, cross_ref, row_ref, sems = refs
        copies = []

        def keeper(held_ref, kept_ref, sems):
            def keep(at, here):
                copy = pltpu.make_async_copy(held_ref.at[here, :], kept_ref.at[here, :], sems.at[at])
                copy.start()
                copies.append(copy)

            return keep

        score_units(
            group_refs[own_from:], [src_ref], cross_ref, row_ref, keeper(cross_ref, kept_ref, sems)
        )
        if parts:
            keep = keeper(faced_cross, faced_kept, faced_sems)
            score_units(group_refs, faced_refs, faced_cross, faced_row, keep)
            faced_lse[...] = log_sum2(faced_row[...])
        lse_ref[...] = log_sum2(row_ref[...])
        for copy in copies:
            copy.wait()

    out_shape = [
        pltpu.HBM((own_rows, HALF), jnp.float32),
        jax.ShapeDtypeStruct((1, HALF), jnp.float32),
    ]
    scratch = [
        pltpu.VMEM((own_rows, HALF), jnp.float32),
        pltpu.VMEM((own_passes, HALF), jnp.float32),
        pltpu.SemaphoreType.DMA((own_passes,)),
    ]
    if parts:
        out_shape += [
            pltpu.HBM((all_rows, width), jnp.float32),
            jax.ShapeDtypeStruct((1, width), jnp.float32),
            jax.ShapeDtypeStruct((1, HALF), jnp.float32),
        ]
        scratch += [
            pltpu.VMEM((all_rows, width), jnp.float32),
            pltpu.VMEM((passes, width), jnp.float32),
            pltpu.SemaphoreType.DMA((passes,)),
        ]
    return pl.pallas_call(
        body,
        in_specs=[IN_VMEM] * (count + 1 + parts),
        out_specs=[IN_HBM, IN_VMEM] + [IN_HBM, IN_VMEM, IN_VMEM] * (parts > 0),
        out_shape=out_shape,
        scratch_shapes=scratch,
        compiler_params=pltpu.CompilerParams(vmem_limit_bytes=VMEM),
        cost_estimate=pl.CostEstimate(flops=1, bytes_accessed=1, transcendentals=0),
        name="rows",
    )(*groups, sources, *faced)


def quarter_places(place_ref):
    return [pl.multiple_of(place_ref[QUARTERS + k] * EDGE, EDGE) for k in range(HALF // EDGE)]


def last_kernel(count, place_ref, *refs):
    group_refs, own_refs, first_refs, round_refs = (
        refs[:count],
        refs[count : count + 1],
        refs[count + 1 : count + 3],
        refs[count + 3 : count + 5],
    )
    first_earlier, *earlier = refs[count + 5 : count + 5 + PASSES]
    near_ref, round_ref, lse_ref, own_row, first_row, round_row = refs[count + 5 + PASSES :]
    score_rows(group_refs[-1:], own_refs, near_ref.at[:, :HALF], own_row)
    score_rows(group_refs[-1:], first_refs, near_ref.at[:, HALF:], first_row)
    score_units(group_refs, round_refs, round_ref, round_row)
    own = log_sum2(jnp.concatenate([own_row[...], *[ref[...] for ref in earlier]], axis=0))
    faced = [
        log_sum2(jnp.concatenate([first_row[...], first_earlier[...]], axis=0)),
        log_sum2(round_row[...]),
    ]
    mine = pl.multiple_of(place_ref[X_HI] * HALF, HALF)
    other = pl.multiple_of((1 - place_ref[X_HI]) * HALF, HALF)
    places = quarter_places(place_ref)
    for peer in range(PEERS):
        lse_ref[peer, :, pl.ds(mine, HALF)] = own
        for at, start in enumerate(places):
            part = faced[at // 2][:, at % 2 * EDGE : (at % 2 + 1) * EDGE]
            lse_ref[peer, :, pl.ds(other + start, EDGE)] = part


def last_pass(place, groups, sources, faced, first_earlier, earlier):
    count = len(groups)
    work = UNIT * (HALF + PART) + ROWS * PART

    def body(*refs):
        last_kernel(count, *refs)

    return pl.pallas_call(
        body,
        in_specs=[IN_SMEM] + [IN_VMEM] * (count + 6 + len(earlier)),
        out_specs=[IN_VMEM] * 3,
        out_shape=[
            pltpu.VMEM((UNIT, HALF + PART), jnp.float32),
            pltpu.VMEM((ROWS, PART), jnp.float32),
            pltpu.VMEM((PEERS, 1, 2 * HALF), jnp.float32),
        ],
        scratch_shapes=[
            pltpu.VMEM((1, HALF), jnp.float32),
            pltpu.VMEM((1, PART), jnp.float32),
            pltpu.VMEM(((count + 1) // 2, PART), jnp.float32),
        ],
        compiler_params=pltpu.CompilerParams(vmem_limit_bytes=VMEM),
        cost_estimate=pl.CostEstimate(
            flops=2 * work * D, bytes_accessed=HALF * D * 4 + work * 4, transcendentals=work
        ),
        name="last_rows",
    )(place, *groups, sources, *faced, first_earlier, *earlier)


def column_kernel(heights, place_ref, *refs):
    own_kept, refs = refs[: len(heights)], refs[len(heights) :]
    first_kept, near_ref, round_ref, partial_ref, sq_ref, logw_ref, faced_logw_ref = refs[:7]
    out_ref, pot_ref, own_held, first_held, peak_ref, total_ref, sems = refs[7:]
    copies, top = [], 0
    for height, own_ref in zip(heights, own_kept):
        for start in range(0, height, UNIT):
            here = slice(top, top + UNIT)
            at = len(copies)
            copies.append(
                (
                    pltpu.make_async_copy(
                        own_ref.at[start : start + UNIT, :], own_held.at[here, :], sems.at[0, at]
                    ),
                    pltpu.make_async_copy(
                        first_kept.at[here, :], first_held.at[here, :], sems.at[1, at]
                    ),
                )
            )
            top += UNIT
    for pair in copies:
        for copy in pair:
            copy.start()
    z, core = place_ref[Z], place_ref[CORE]
    mine = pl.multiple_of(place_ref[X_HI] * HALF, HALF)
    other = pl.multiple_of((1 - place_ref[X_HI]) * HALF, HALF)
    row = log_sum2(partial_ref[:, 0, pl.ds(mine, HALF)])
    own_bias = logw_ref[...] * LOG2E - row
    pot_ref[...] = sq_ref[...] - BACK * row
    own_bias = jnp.broadcast_to(own_bias, (8, HALF))
    faced_bias = [
        faced_logw_ref[:, pl.ds(start, EDGE)] * LOG2E
        - log_sum2(partial_ref[:, 0, pl.ds(other + start, EDGE)])
        for start in quarter_places(place_ref)
    ]
    first_bias = jnp.broadcast_to(jnp.concatenate(faced_bias[:2], axis=1), (8, PART))
    round_bias = jnp.broadcast_to(jnp.concatenate(faced_bias[2:], axis=1), (8, PART))

    def lanes(values):
        return [values[:, k : k + LANES] for k in range(0, values.shape[1], LANES)]

    def sums(pieces, before=None):
        peak = pieces[0] if before is None else jnp.maximum(before[0], pieces[0])
        for piece in pieces[1:]:
            peak = jnp.maximum(peak, piece)
        total = jnp.exp2(pieces[0] - peak)
        for piece in pieces[1:]:
            total = total + jnp.exp2(piece - peak)
        if before is not None:
            total = total + before[1] * jnp.exp2(before[0] - peak)
        return peak, total

    last = REST
    for at in range(0, ROWS, 8):
        rows = slice(at, at + 8)
        pieces = lanes(round_ref[rows, :] + round_bias)
        if at >= last:
            near = near_ref[at - last : at - last + 8, :]
            pieces += lanes(near[:, :HALF] + own_bias) + lanes(near[:, HALF:] + first_bias)
        peak_ref[rows, :], total_ref[rows, :] = sums(pieces)
    for units in (range(2), range(2, 4), range(4, UNITS - 1)):
        for unit in units:
            for copy in copies[unit]:
                copy.wait()
        for at in range(units.start * UNIT, units.stop * UNIT, 8):
            rows = slice(at, at + 8)
            pieces = lanes(own_held[rows, :] + own_bias)
            pieces += lanes(first_held[rows, :] + first_bias)
            before = peak_ref[rows, :], total_ref[rows, :]
            peak_ref[rows, :], total_ref[rows, :] = sums(pieces, before)
    side = 1 - 2 * core
    for unit in range(UNITS):
        rows = slice(unit * UNIT, (unit + 1) * UNIT)
        peak, total = peak_ref[rows, :].T, total_ref[rows, :].T
        highest = jnp.max(peak, axis=0, keepdims=True)
        total = jnp.sum(total * jnp.exp2(peak - highest), axis=0, keepdims=True)
        lse = highest + jnp.log2(total)
        if unit == 0:
            first, second = 2 * z + core, 2 * z + 1 - core
        else:
            step = (unit + 1) // 2
            chip = lax.rem(z + UNITS + (side if unit % 2 else -side) * step, UNITS)
            first, second = 2 * chip, 2 * chip + 1
        out_ref[pl.ds(first, 1)] = lse[:, :OWN].reshape(1, 1, OWN)
        out_ref[pl.ds(second, 1)] = lse[:, OWN:].reshape(1, 1, OWN)


def column_pass(place, own_crosses, first_cross, near, round_cross, partial, *rows):
    heights = [cross.shape[0] for cross in own_crosses]

    def body(*refs):
        column_kernel(heights, *refs)

    return pl.pallas_call(
        body,
        in_specs=[IN_SMEM] + [IN_HBM] * (len(own_crosses) + 1) + [IN_VMEM] * 6,
        out_specs=[IN_VMEM] * 2,
        out_shape=[
            jax.ShapeDtypeStruct((PEERS, 1, OWN), jnp.float32),
            jax.ShapeDtypeStruct((1, HALF), jnp.float32),
        ],
        scratch_shapes=[
            pltpu.VMEM((REST, HALF), jnp.float32),
            pltpu.VMEM((REST, PART), jnp.float32),
            pltpu.VMEM((ROWS, LANES), jnp.float32),
            pltpu.VMEM((ROWS, LANES), jnp.float32),
            pltpu.SemaphoreType.DMA((2, UNITS - 1)),
        ],
        compiler_params=pltpu.CompilerParams(vmem_limit_bytes=VMEM),
        cost_estimate=pl.CostEstimate(
            flops=12 * ROWS * HALF, bytes_accessed=ROWS * HALF * 8, transcendentals=2 * ROWS * HALF
        ),
        name="columns",
    )(
        place,
        *in_hbm(*own_crosses, first_cross),
        pltpu.with_memory_space_constraint(near, pltpu.VMEM),
        pltpu.with_memory_space_constraint(round_cross, pltpu.VMEM),
        partial,
        *[row.reshape(1, HALF) for row in rows],
    )


def on_device(sources, targets, potential_in, source_logw, target_logw):
    x_lo, x_hi, odd = lax.axis_index("x_lo"), lax.axis_index("x_hi"), lax.axis_index("y") % 2
    quarters = [
        2 * odd + x_lo,
        2 * (1 - odd) + 1 - x_lo,
        2 * (1 - odd) + x_lo,
        2 * odd + 1 - x_lo,
    ]
    sent, sent_next = 2 * odd + 1 - x_lo, 2 * (1 - odd) + x_lo
    place = jnp.stack(
        [x_hi, lax.axis_index("z"), lax.axis_index("core"), *quarters, sent]
    ).astype(jnp.int32)
    own, tgt_sq, edge = pack(
        place, sources, targets, potential_in, target_logw, source_logw
    )
    straight = facing(edge)
    same, cross_core = onward(own), onward_across(own)
    opposite = facing(lax.dynamic_slice(sources, (sent_next * EDGE, 0), (EDGE, D)))
    beside = other_core(own)

    first = lax.axis_index("core") == 0
    unit = jnp.concatenate(
        [jnp.where(first, same, cross_core), jnp.where(first, cross_core, same)], axis=0
    )
    src_sq = jnp.sum(jnp.square(sources.astype(jnp.float32)), axis=1)
    groups, crosses, lses = [own, beside], [], []
    for step in (1, 2):
        following = onward(unit)
        beside = other_core(unit)
        if step == 1:
            by_y, by_x = beside_y(straight), beside_x(straight)
        cross, lse = row_pass(groups[-2:], sources)
        crosses.append(cross)
        lses.append(lse)
        groups += [unit, beside]
        if step == 1:
            unit, lses[0], src_sq = lax.optimization_barrier((following, lse, src_sq))
        else:
            unit, lses[1] = lax.optimization_barrier((following, lse))
            groups[-1], opposite = lax.optimization_barrier((groups[-1], opposite))
    groups += [unit, other_core(unit)]
    following = onward(unit)
    cross, lse, first_cross, first_lse, faced_logw = row_pass(
        groups, sources, [straight, opposite], 4
    )
    crosses.append(cross)
    unit, lse, first_lse = lax.optimization_barrier((following, lse, first_lse))
    lses.append(lse)
    groups.append(unit)
    near, round_cross, shared = last_pass(
        place, groups, sources, [straight, opposite, by_y, by_x], first_lse, lses
    )

    partial = lax.all_to_all(shared, ("y", "x_lo", "x_hi"), 0, 0, tiled=True)
    columns, source_potential = column_pass(
        place, crosses, first_cross, near, round_cross, partial, src_sq, source_logw, faced_logw
    )
    gathered = lax.all_to_all(columns, ("z", "core"), 0, 0, tiled=True)
    final = log_sum2(gathered.reshape(PEERS, OWN)).reshape(OWN)
    potential_out = tgt_sq.reshape(OWN) - BACK * final
    return (source_potential.reshape(HALF), potential_out)


def solution(mesh):
    every = ("y", "x_lo", "z", "x_hi", "core")
    blk = ("z", "x_hi", "core")
    fine = Mesh(mesh.devices.reshape(4, 2, 8, 2, 2), every)
    in_specs = (P(blk, None), P(every, None), P(every), P(blk), P(every))
    out_specs = (P(blk), P(every))
    return jax.shard_map(
        on_device, mesh=fine, in_specs=in_specs, out_specs=out_specs, check_vma=False
    )
```

```python
import math

import jax
import jax.numpy as jnp
from jax import lax
from jax.experimental import pallas as pl
from jax.experimental.pallas import tpu as pltpu
from jax.sharding import Mesh, PartitionSpec as P

EPSILON = 0.05
LOG2E = math.log2(math.e)
SCALE = 2.0 / EPSILON * LOG2E
BACK = EPSILON * math.log(2.0)

D = 768
PAD = 128
OWN = 64
UNIT = 2 * OWN
UNITS = 8
ROWS = UNIT * UNITS
HALF = 1024
BLOCK = 512
LANES = 128
PEERS = 16
X_HI, Z, CORE, QUARTERS, SENT = 0, 1, 2, 3, 7
PART = HALF // 2
PASSES = 4
VMEM = 12 * 1024 * 1024
EDGE = HALF // 4
EXTRA = 16
REST = ROWS - UNIT
IN_VMEM = pl.BlockSpec(memory_space=pltpu.VMEM)
IN_HBM = pl.BlockSpec(memory_space=pl.ANY)
IN_SMEM = pl.BlockSpec(memory_space=pltpu.SMEM)


def whole(*shape):
    return pl.BlockSpec(shape, lambda i: (0,) * len(shape))


def onward(value):
    count = lax.axis_size("z")
    up = [(2 * i + 1, 2 * ((i + 1) % count) + 1) for i in range(count)]
    down = [(2 * i, 2 * ((i - 1) % count)) for i in range(count)]
    return lax.ppermute(value, ("z", "core"), up + down)


def onward_across(value):
    count = lax.axis_size("z")
    up = [(2 * i, 2 * ((i + 1) % count) + 1) for i in range(count)]
    down = [(2 * i + 1, 2 * ((i - 1) % count)) for i in range(count)]
    return lax.ppermute(value, ("z", "core"), up + down)


def other_core(value):
    return lax.ppermute(value, "core", [(0, 1), (1, 0)])


def facing(value):
    return lax.ppermute(value, ("x_lo", "x_hi"), [(0, 3), (3, 0), (1, 2), (2, 1)])


def beside_x(value):
    return lax.ppermute(value, "x_lo", [(0, 1), (1, 0)])


def beside_y(value):
    return lax.ppermute(value, "y", [(0, 1), (1, 0), (2, 3), (3, 2)])


def log_sum2(values):
    peak = jnp.max(values, axis=0, keepdims=True)
    return peak + jnp.log2(jnp.sum(jnp.exp2(values - peak), axis=0, keepdims=True))


def split(values):
    high = values.astype(jnp.bfloat16).astype(jnp.float32)
    rest = values - high
    middle = rest.astype(jnp.bfloat16).astype(jnp.float32)
    return high, middle, rest - middle


def pack_kernel(place_ref, src_hbm, tgt_hbm, pot_hbm, logw_hbm, *refs):
    src_logw_hbm, own_ref, sq_ref, edge_ref, tgt_ref, pot_ref, logw_ref, src_logw_ref, sems = refs
    copies = [
        pltpu.make_async_copy(source, target, sems.at[at])
        for at, (source, target) in enumerate(
            (
                (tgt_hbm, tgt_ref),
                (pot_hbm, pot_ref),
                (logw_hbm, logw_ref),
                (src_logw_hbm, src_logw_ref),
            )
        )
    ]
    for copy in copies:
        copy.start()
    start = pl.multiple_of(place_ref[SENT] * EDGE, EDGE)
    edge = pltpu.make_async_copy(
        src_hbm.at[pl.ds(start, EDGE), :], edge_ref.at[:EDGE, :], sems.at[4]
    )
    edge.start()
    for copy in copies:
        copy.wait()
    tgt = tgt_ref[...]
    wide = tgt.astype(jnp.float32)
    sq = jnp.sum(wide * wide, axis=1, keepdims=True)
    diagonal = lax.broadcasted_iota(jnp.int32, (OWN, OWN), 0) == lax.broadcasted_iota(
        jnp.int32, (OWN, OWN), 1
    )

    def upright(row):
        return jnp.sum(jnp.where(diagonal, row, 0.0), axis=1, keepdims=True)

    sq_ref[...] = jnp.sum(jnp.where(diagonal, sq, 0.0), axis=0, keepdims=True)
    bias = (upright(logw_ref[...]) + (upright(pot_ref[...]) - sq) / EPSILON) * LOG2E
    high, middle, low = split(bias)
    lane = lax.broadcasted_iota(jnp.int32, (OWN, PAD), 1)
    pieces = jnp.where(lane == 0, high, 0.0)
    pieces = jnp.where(lane == 1, middle, pieces)
    pieces = jnp.where(lane == 2, low, pieces)
    own_ref[:, :D] = tgt
    own_ref[:, D:] = pieces.astype(jnp.bfloat16)
    line = lax.broadcasted_iota(jnp.int32, (EXTRA, D), 0)
    extra = jnp.zeros((EXTRA, D), jnp.float32)
    for quarter in range(HALF // EDGE):
        part = src_logw_ref[:, quarter * EDGE : (quarter + 1) * EDGE]
        row = jnp.concatenate(split(part), axis=1)
        extra = jnp.where(line == quarter, row, extra)
    edge_ref[EDGE:, :] = extra.astype(jnp.bfloat16)
    edge.wait()


def in_hbm(*values):
    return [pltpu.with_memory_space_constraint(value, pltpu.HBM) for value in values]


def pack(place, sources, targets, potential, logw, src_logw):
    return pl.pallas_call(
        pack_kernel,
        in_specs=[IN_SMEM] + [IN_HBM] * 5,
        out_specs=[IN_VMEM] * 3,
        out_shape=[
            jax.ShapeDtypeStruct((OWN, D + PAD), jnp.bfloat16),
            jax.ShapeDtypeStruct((1, OWN), jnp.float32),
            jax.ShapeDtypeStruct((EDGE + EXTRA, D), jnp.bfloat16),
        ],
        scratch_shapes=[
            pltpu.VMEM((OWN, D), jnp.bfloat16),
            pltpu.VMEM((1, OWN), jnp.float32),
            pltpu.VMEM((1, OWN), jnp.float32),
            pltpu.VMEM((1, HALF), jnp.float32),
            pltpu.SemaphoreType.DMA((5,)),
        ],
        compiler_params=pltpu.CompilerParams(vmem_limit_bytes=VMEM),
        name="pack",
    )(
        place,
        *in_hbm(
            sources,
            targets,
            potential.reshape(1, OWN),
            logw.reshape(1, OWN),
            src_logw.reshape(1, HALF),
        ),
    )


def score_rows(group_refs, src_refs, cross_ref, lse_ref):
    group = jnp.concatenate([ref[...] for ref in group_refs], axis=0)
    pieces = group[:, D:].astype(jnp.float32)
    bias = pieces[:, 0:1] + pieces[:, 1:2] + pieces[:, 2:3]
    group = group[:, :D]
    place, totals = 0, []
    for src_ref in src_refs:
        height = src_ref.shape[0] // EDGE * EDGE
        rows = min(BLOCK, height)
        for start in range(0, height, rows):
            cross = SCALE * lax.dot_general(
                group,
                src_ref[start : start + rows, :],
                (((1,), (1,)), ((), ())),
                preferred_element_type=jnp.float32,
            )
            cross_ref[:, place : place + rows] = cross
            totals.append(log_sum2(cross + bias))
            place += rows
    lse_ref[...] = jnp.concatenate(totals, axis=1)


def score_units(group_refs, src_refs, cross_ref, row_ref, done=None):
    top = 0
    for at in range((len(group_refs) + 1) // 2):
        pair = group_refs[2 * at : 2 * at + 2]
        here = slice(top, top + sum(ref.shape[0] for ref in pair))
        score_rows(pair, src_refs, cross_ref.at[here, :], row_ref.at[at : at + 1, :])
        if done is not None:
            done(at, here)
        top = here.stop


def row_pass(groups, sources, faced=(), late=0):
    count, parts = len(groups), len(faced)
    tops = [sum(group.shape[0] for group in groups[:at]) for at in range(count + 1)]
    own_from = count - late if parts else 0
    own_rows, all_rows = tops[-1] - tops[own_from], tops[-1]
    own_passes, passes = (count - own_from + 1) // 2, (count + 1) // 2
    width = sum(part.shape[0] // EDGE * EDGE for part in faced)

    def body(*refs):
        group_refs, src_ref = refs[:count], refs[count]
        faced_refs, refs = refs[count + 1 : count + 1 + parts], refs[count + 1 + parts :]
        if parts:
            kept_ref, lse_ref, faced_kept, faced_lse, logw_ref, *refs = refs
            cross_ref, row_ref, sems, faced_cross, faced_row, faced_sems = refs
            extra = faced_refs[0][EDGE:, :].astype(jnp.float32)
            sums = extra[:, :EDGE] + extra[:, EDGE : 2 * EDGE] + extra[:, 2 * EDGE :]
            for quarter in range(HALF // EDGE):
                here = slice(quarter * EDGE, (quarter + 1) * EDGE)
                logw_ref[:, here] = sums[quarter : quarter + 1, :]
        else:
            kept_ref, lse_ref, cross_ref, row_ref, sems = refs
        copies = []

        def keeper(held_ref, kept_ref, sems):
            def keep(at, here):
                copy = pltpu.make_async_copy(held_ref.at[here, :], kept_ref.at[here, :], sems.at[at])
                copy.start()
                copies.append(copy)

            return keep

        score_units(
            group_refs[own_from:], [src_ref], cross_ref, row_ref, keeper(cross_ref, kept_ref, sems)
        )
        if parts:
            keep = keeper(faced_cross, faced_kept, faced_sems)
            score_units(group_refs, faced_refs, faced_cross, faced_row, keep)
            faced_lse[...] = log_sum2(faced_row[...])
        lse_ref[...] = log_sum2(row_ref[...])
        for copy in copies:
            copy.wait()

    out_shape = [
        pltpu.HBM((own_rows, HALF), jnp.float32),
        jax.ShapeDtypeStruct((1, HALF), jnp.float32),
    ]
    scratch = [
        pltpu.VMEM((own_rows, HALF), jnp.float32),
        pltpu.VMEM((own_passes, HALF), jnp.float32),
        pltpu.SemaphoreType.DMA((own_passes,)),
    ]
    if parts:
        out_shape += [
            pltpu.HBM((all_rows, width), jnp.float32),
            jax.ShapeDtypeStruct((1, width), jnp.float32),
            jax.ShapeDtypeStruct((1, HALF), jnp.float32),
        ]
        scratch += [
            pltpu.VMEM((all_rows, width), jnp.float32),
            pltpu.VMEM((passes, width), jnp.float32),
            pltpu.SemaphoreType.DMA((passes,)),
        ]
    return pl.pallas_call(
        body,
        in_specs=[IN_VMEM] * (count + 1 + parts),
        out_specs=[IN_HBM, IN_VMEM] + [IN_HBM, IN_VMEM, IN_VMEM] * (parts > 0),
        out_shape=out_shape,
        scratch_shapes=scratch,
        compiler_params=pltpu.CompilerParams(vmem_limit_bytes=VMEM),
        cost_estimate=pl.CostEstimate(flops=1, bytes_accessed=1, transcendentals=0),
        name="rows",
    )(*groups, sources, *faced)


def quarter_places(place_ref):
    return [pl.multiple_of(place_ref[QUARTERS + k] * EDGE, EDGE) for k in range(HALF // EDGE)]


def last_kernel(count, place_ref, *refs):
    group_refs, own_refs, first_refs, round_refs = (
        refs[:count],
        refs[count : count + 1],
        refs[count + 1 : count + 3],
        refs[count + 3 : count + 5],
    )
    first_earlier, *earlier = refs[count + 5 : count + 5 + PASSES]
    near_ref, round_ref, lse_ref, own_row, first_row, round_row = refs[count + 5 + PASSES :]
    score_rows(group_refs[-1:], own_refs, near_ref.at[:, :HALF], own_row)
    score_rows(group_refs[-1:], first_refs, near_ref.at[:, HALF:], first_row)
    score_units(group_refs, round_refs, round_ref, round_row)
    own = log_sum2(jnp.concatenate([own_row[...], *[ref[...] for ref in earlier]], axis=0))
    faced = [
        log_sum2(jnp.concatenate([first_row[...], first_earlier[...]], axis=0)),
        log_sum2(round_row[...]),
    ]
    mine = pl.multiple_of(place_ref[X_HI] * HALF, HALF)
    other = pl.multiple_of((1 - place_ref[X_HI]) * HALF, HALF)
    places = quarter_places(place_ref)
    for peer in range(PEERS):
        lse_ref[peer, :, pl.ds(mine, HALF)] = own
        for at, start in enumerate(places):
            part = faced[at // 2][:, at % 2 * EDGE : (at % 2 + 1) * EDGE]
            lse_ref[peer, :, pl.ds(other + start, EDGE)] = part


def last_pass(place, groups, sources, faced, first_earlier, earlier):
    count = len(groups)
    work = UNIT * (HALF + PART) + ROWS * PART

    def body(*refs):
        last_kernel(count, *refs)

    return pl.pallas_call(
        body,
        in_specs=[IN_SMEM] + [IN_VMEM] * (count + 6 + len(earlier)),
        out_specs=[IN_VMEM] * 3,
        out_shape=[
            pltpu.VMEM((UNIT, HALF + PART), jnp.float32),
            pltpu.VMEM((ROWS, PART), jnp.float32),
            pltpu.VMEM((PEERS, 1, 2 * HALF), jnp.float32),
        ],
        scratch_shapes=[
            pltpu.VMEM((1, HALF), jnp.float32),
            pltpu.VMEM((1, PART), jnp.float32),
            pltpu.VMEM(((count + 1) // 2, PART), jnp.float32),
        ],
        compiler_params=pltpu.CompilerParams(vmem_limit_bytes=VMEM),
        cost_estimate=pl.CostEstimate(
            flops=2 * work * D, bytes_accessed=HALF * D * 4 + work * 4, transcendentals=work
        ),
        name="last_rows",
    )(place, *groups, sources, *faced, first_earlier, *earlier)


def column_kernel(heights, place_ref, *refs):
    own_kept, refs = refs[: len(heights)], refs[len(heights) :]
    first_kept, near_ref, round_ref, partial_ref, sq_ref, logw_ref, faced_logw_ref = refs[:7]
    out_ref, pot_ref, own_held, first_held, peak_ref, total_ref, sems = refs[7:]
    copies, top = [], 0
    for height, own_ref in zip(heights, own_kept):
        for start in range(0, height, UNIT):
            here = slice(top, top + UNIT)
            at = len(copies)
            copies.append(
                (
                    pltpu.make_async_copy(
                        own_ref.at[start : start + UNIT, :], own_held.at[here, :], sems.at[0, at]
                    ),
                    pltpu.make_async_copy(
                        first_kept.at[here, :], first_held.at[here, :], sems.at[1, at]
                    ),
                )
            )
            top += UNIT
    for pair in copies:
        for copy in pair:
            copy.start()
    z, core = place_ref[Z], place_ref[CORE]
    mine = pl.multiple_of(place_ref[X_HI] * HALF, HALF)
    other = pl.multiple_of((1 - place_ref[X_HI]) * HALF, HALF)
    row = log_sum2(partial_ref[:, 0, pl.ds(mine, HALF)])
    own_bias = logw_ref[...] * LOG2E - row
    pot_ref[...] = sq_ref[...] - BACK * row
    own_bias = jnp.broadcast_to(own_bias, (8, HALF))
    faced_bias = [
        faced_logw_ref[:, pl.ds(start, EDGE)] * LOG2E
        - log_sum2(partial_ref[:, 0, pl.ds(other + start, EDGE)])
        for start in quarter_places(place_ref)
    ]
    first_bias = jnp.broadcast_to(jnp.concatenate(faced_bias[:2], axis=1), (8, PART))
    round_bias = jnp.broadcast_to(jnp.concatenate(faced_bias[2:], axis=1), (8, PART))

    def lanes(values):
        return [values[:, k : k + LANES] for k in range(0, values.shape[1], LANES)]

    def sums(pieces, before=None):
        peak = pieces[0] if before is None else jnp.maximum(before[0], pieces[0])
        for piece in pieces[1:]:
            peak = jnp.maximum(peak, piece)
        total = jnp.exp2(pieces[0] - peak)
        for piece in pieces[1:]:
            total = total + jnp.exp2(piece - peak)
        if before is not None:
            total = total + before[1] * jnp.exp2(before[0] - peak)
        return peak, total

    last = REST
    for at in range(0, ROWS, 8):
        rows = slice(at, at + 8)
        pieces = lanes(round_ref[rows, :] + round_bias)
        if at >= last:
            near = near_ref[at - last : at - last + 8, :]
            pieces += lanes(near[:, :HALF] + own_bias) + lanes(near[:, HALF:] + first_bias)
        peak_ref[rows, :], total_ref[rows, :] = sums(pieces)
    for units in (range(2), range(2, 4), range(4, UNITS - 1)):
        for unit in units:
            for copy in copies[unit]:
                copy.wait()
        for at in range(units.start * UNIT, units.stop * UNIT, 8):
            rows = slice(at, at + 8)
            pieces = lanes(own_held[rows, :] + own_bias)
            pieces += lanes(first_held[rows, :] + first_bias)
            before = peak_ref[rows, :], total_ref[rows, :]
            peak_ref[rows, :], total_ref[rows, :] = sums(pieces, before)
    side = 1 - 2 * core
    for unit in range(UNITS):
        rows = slice(unit * UNIT, (unit + 1) * UNIT)
        peak, total = peak_ref[rows, :].T, total_ref[rows, :].T
        highest = jnp.max(peak, axis=0, keepdims=True)
        total = jnp.sum(total * jnp.exp2(peak - highest), axis=0, keepdims=True)
        lse = highest + jnp.log2(total)
        if unit == 0:
            first, second = 2 * z + core, 2 * z + 1 - core
        else:
            step = (unit + 1) // 2
            chip = lax.rem(z + UNITS + (side if unit % 2 else -side) * step, UNITS)
            first, second = 2 * chip, 2 * chip + 1
        out_ref[pl.ds(first, 1)] = lse[:, :OWN].reshape(1, 1, OWN)
        out_ref[pl.ds(second, 1)] = lse[:, OWN:].reshape(1, 1, OWN)


def column_pass(place, own_crosses, first_cross, near, round_cross, partial, *rows):
    heights = [cross.shape[0] for cross in own_crosses]

    def body(*refs):
        column_kernel(heights, *refs)

    return pl.pallas_call(
        body,
        in_specs=[IN_SMEM] + [IN_HBM] * (len(own_crosses) + 1) + [IN_VMEM] * 6,
        out_specs=[IN_VMEM] * 2,
        out_shape=[
            jax.ShapeDtypeStruct((PEERS, 1, OWN), jnp.float32),
            jax.ShapeDtypeStruct((1, HALF), jnp.float32),
        ],
        scratch_shapes=[
            pltpu.VMEM((REST, HALF), jnp.float32),
            pltpu.VMEM((REST, PART), jnp.float32),
            pltpu.VMEM((ROWS, LANES), jnp.float32),
            pltpu.VMEM((ROWS, LANES), jnp.float32),
            pltpu.SemaphoreType.DMA((2, UNITS - 1)),
        ],
        compiler_params=pltpu.CompilerParams(vmem_limit_bytes=VMEM),
        cost_estimate=pl.CostEstimate(
            flops=12 * ROWS * HALF, bytes_accessed=ROWS * HALF * 8, transcendentals=2 * ROWS * HALF
        ),
        name="columns",
    )(
        place,
        *in_hbm(*own_crosses, first_cross),
        pltpu.with_memory_space_constraint(near, pltpu.VMEM),
        pltpu.with_memory_space_constraint(round_cross, pltpu.VMEM),
        partial,
        *[row.reshape(1, HALF) for row in rows],
    )


def on_device(sources, targets, potential_in, source_logw, target_logw):
    x_lo, x_hi, odd = lax.axis_index("x_lo"), lax.axis_index("x_hi"), lax.axis_index("y") % 2
    quarters = [
        2 * odd + x_lo,
        2 * (1 - odd) + 1 - x_lo,
        2 * (1 - odd) + x_lo,
        2 * odd + 1 - x_lo,
    ]
    sent, sent_next = 2 * odd + 1 - x_lo, 2 * (1 - odd) + x_lo
    place = jnp.stack(
        [x_hi, lax.axis_index("z"), lax.axis_index("core"), *quarters, sent]
    ).astype(jnp.int32)
    own, tgt_sq, edge = pack(
        place, sources, targets, potential_in, target_logw, source_logw
    )
    straight = facing(edge)
    same, cross_core = onward(own), onward_across(own)
    opposite = facing(lax.dynamic_slice(sources, (sent_next * EDGE, 0), (EDGE, D)))
    beside = other_core(own)

    first = lax.axis_index("core") == 0
    unit = jnp.concatenate(
        [jnp.where(first, same, cross_core), jnp.where(first, cross_core, same)], axis=0
    )
    src_sq = jnp.sum(jnp.square(sources.astype(jnp.float32)), axis=1)
    groups, crosses, lses = [own, beside], [], []
    for step in (1, 2):
        following = onward(unit)
        beside = other_core(unit)
        if step == 1:
            by_y, by_x = beside_y(straight), beside_x(straight)
        cross, lse = row_pass(groups[-2:], sources)
        crosses.append(cross)
        lses.append(lse)
        groups += [unit, beside]
        if step == 1:
            unit, lses[0], src_sq = lax.optimization_barrier((following, lse, src_sq))
        else:
            unit, lses[1] = lax.optimization_barrier((following, lse))
    following = onward(unit)
    swapped = other_core(unit)
    swapped, opposite = lax.optimization_barrier((swapped, opposite))
    groups += [unit, swapped]
    cross, lse, first_cross, first_lse, faced_logw = row_pass(
        groups, sources, [straight, opposite], 4
    )
    crosses.append(cross)
    unit, lse, first_lse = lax.optimization_barrier((following, lse, first_lse))
    lses.append(lse)
    groups.append(unit)
    near, round_cross, shared = last_pass(
        place, groups, sources, [straight, opposite, by_y, by_x], first_lse, lses
    )

    partial = lax.all_to_all(shared, ("y", "x_lo", "x_hi"), 0, 0, tiled=True)
    columns, source_potential = column_pass(
        place, crosses, first_cross, near, round_cross, partial, src_sq, source_logw, faced_logw
    )
    gathered = lax.all_to_all(columns, ("z", "core"), 0, 0, tiled=True)
    final = log_sum2(gathered.reshape(PEERS, OWN)).reshape(OWN)
    potential_out = tgt_sq.reshape(OWN) - BACK * final
    return (source_potential.reshape(HALF), potential_out)


def solution(mesh):
    every = ("y", "x_lo", "z", "x_hi", "core")
    blk = ("z", "x_hi", "core")
    fine = Mesh(mesh.devices.reshape(4, 2, 8, 2, 2), every)
    in_specs = (P(blk, None), P(every, None), P(every), P(blk), P(every))
    out_specs = (P(blk), P(every))
    return jax.shard_map(
        on_device, mesh=fine, in_specs=in_specs, out_specs=out_specs, check_vma=False
    )
```
